768 devices in a mesh: group: 16 (over z_hi, x, core), shard: 48 (over y, z_lo).
Axes of the slice: x: 4, y: 8, z: 12 (z_hi: 2, z_lo: 6; z = z_hi * 6 + z_lo), core: 2. Of those that a mesh axis runs over, the one named last changes fastest.
Arguments:
- table: float32 [16, 48, 1024, 256], P('group', 'shard'), may hold values from -0.6 to 0.6
- row_state: float32 [16, 48, 1024], P('group', 'shard'), may hold values from 0.1 to 1
- bag_ids: int32 [16, 48, 4, 1536], P('group', 'shard'), may hold values from 0 to 1023
- bag_lengths: int32 [16, 48, 1536], P('group', 'shard'), may hold values from 1 to 4, as said below
- interaction_grad: float32 [16, 48, 48, 1536], P('group', None, None, 'shard'), may hold values from -0.875 to 0.875
- move_rows: int32 [16, 48, 16], P('group', 'shard'), may hold values from 0 to 64, as said below
Outputs:
- new_table: float32 [16, 48, 1024, 256], P('group', 'shard')
- new_state: float32 [16, 48, 1024], P('group', 'shard')
- arrived: float32 [16, 16, 48, 64, 256], P('group', None, 'shard')
- arrived_state: float32 [16, 16, 48, 64], P('group', None, 'shard')
The draws below stay inside these ranges and needn't reach their ends.
Inputs may be any that keep to these rules, and one draw needn't show every extreme that they name: `bag_lengths`: in every table shard some bag has exactly 4 live slots. `move_rows`: every table shard sends exactly 64 rows to at least one group; its rows sent add up to at most 1024.
All inputs are finite; a program needn't handle non-finite values.
Results may differ from the reference program's by a relative error of at most 0.0009.
Values may be sent and summed in bfloat16 or wider, within the bound.
A program may use at most 32 MiB of HBM per device.

```python
import math
import jax
import jax.numpy as jnp
import numpy as np
from jax import lax

E = 256
ROWS = 1024
BAG = 4
CAP = 64
SAMPLES = 1536
N_GROUP = 16
N_SHARD = 48


def draw_bag_lengths(key, part):
    key = jax.random.fold_in(key, 11)
    first, second = jax.random.split(key)
    values = jax.random.randint(first, (N_GROUP, N_SHARD, SAMPLES), 1, BAG + 1)
    places = jax.random.randint(second, (N_GROUP, N_SHARD, 1), 0, SAMPLES)
    column = jnp.arange(SAMPLES, dtype=jnp.int32)[None, None, :]
    return jnp.where(column == places, BAG, values).astype(jnp.int32)


def draw_move_rows(key, part):
    key = jax.random.fold_in(key, 23)
    first, second = jax.random.split(key)
    values = jax.random.randint(first, (N_GROUP, N_SHARD, N_GROUP), 0, CAP + 1)
    heavy = jax.random.randint(second, (N_GROUP, N_SHARD, 1), 0, N_GROUP)
    column = jnp.arange(N_GROUP, dtype=jnp.int32)[None, None, :]
    return jnp.where(column == heavy, CAP, values).astype(jnp.int32)


def with_ends(array, stream_key, least, top_value):
    longest = array.shape.index(max(array.shape))
    spots = []
    for shift in (0, 1):
        where = [jax.random.randint(jax.random.fold_in(stream_key, axis), (), 0, length) for axis, length in enumerate(array.shape)]
        where[longest] = (where[longest] + shift) % array.shape[longest]
        spots.append(tuple(where))
    return array.at[spots[0]].set(least).at[spots[1]].set(top_value)


def levels(key, extent, cuts, low, high):
    def one(axis_at, blocks):
        steps = jax.random.uniform(jax.random.fold_in(jax.random.fold_in(key, 6), axis_at), (blocks,), jnp.float32, low / len(cuts), high / len(cuts))
        return jnp.repeat(jnp.exp(steps), extent[axis_at] // blocks).reshape((-1,) + (1,) * (len(extent) - axis_at - 1))

    factor_of = one(*cuts[0])
    for cut in cuts[1:]:
        factor_of = factor_of * one(*cut)
    return factor_of


def rank_table(count, lean):
    loads = [(1 << 20) // math.isqrt(standing ** lean) + 1 for standing in range(1, count + 1)]
    spread = 1 + sum(loads) // (1 << 30)
    return np.cumsum(np.array([max(1, weight // spread) for weight in loads]))


def ranked_ids(rng, shape, number_of, skew):
    listing = rank_table(number_of, skew)
    ticket = jax.random.randint(jax.random.fold_in(rng, 1), shape, 0, int(listing[number_of - 1]))
    rank = jnp.searchsorted(jnp.asarray(listing, jnp.int32), ticket, side="right")
    return jax.random.permutation(jax.random.fold_in(rng, 2), number_of)[rank].astype(jnp.int32)


def scatter_about(own_key, extent, scale, reach, cuts=(), kind=jnp.bfloat16):
    level = levels(own_key, extent, cuts, -0.22, 0.18) if cuts else 1.0
    array = jax.random.normal(own_key, extent, jnp.float32) * scale * level
    return jnp.minimum(jnp.maximum(array, -reach), reach).astype(kind)


def setup_inputs(seed: int = 0) -> dict:
    keys = jax.random.split(jax.random.key(seed), 7)
    return {
        "table": scatter_about(keys[0], (N_GROUP, N_SHARD, ROWS, E), 0.1, 0.6, ((0, 16), (1, 48)), jnp.float32),
        "row_state": jnp.clip(jnp.exp(math.log(1.0) - 2.3025851 * jax.random.uniform(keys[1], (N_GROUP, N_SHARD, ROWS), jnp.float32) ** levels(keys[1], (N_GROUP, N_SHARD, ROWS), ((0, 16), (1, 48)), -0.2, 0.2)), 0.1, 1.0),
        "bag_ids": with_ends(ranked_ids(keys[2], (N_GROUP, N_SHARD, BAG, SAMPLES), ROWS, 2), jax.random.fold_in(keys[2], 3), 0, ROWS - 1).astype(jnp.int32),
        "bag_lengths": draw_bag_lengths(jax.random.fold_in(keys[6], 71), 0),
        "interaction_grad": scatter_about(keys[4], (N_GROUP, N_SHARD, N_SHARD, SAMPLES), N_SHARD ** -0.5, 0.875, ((0, 16), (3, 48)), jnp.float32),
        "move_rows": draw_move_rows(jax.random.fold_in(keys[6], 71), 0),
    }


learn_rate = 0.05
epsilon = 1e-08

def pool_table(rows_table, bag_rows, bag_len):

    def add_slot(bag_slot, running):
        picked = rows_table[bag_rows[bag_slot]]
        return running + jnp.where((bag_slot < bag_len)[:, None], picked, 0.0)
    initial = jnp.zeros((bag_rows.shape[1], rows_table.shape[1]), jnp.float32)
    return lax.fori_loop(0, bag_rows.shape[0], add_slot, initial)

def row_gradients(num_rows, bag_rows, bag_len, upstream_rows):
    grad_values = upstream_rows.astype(jnp.float32)

    def add_slot(bag_slot, running):
        masked = jnp.where((bag_slot < bag_len)[:, None], grad_values, 0.0)
        return running.at[bag_rows[bag_slot]].add(masked)
    initial = jnp.zeros((num_rows, upstream_rows.shape[1]), jnp.float32)
    return lax.fori_loop(0, bag_rows.shape[0], add_slot, initial)

def adagrad(rows_table, state_rows, row_grads):
    new_state = state_rows + lax.optimization_barrier(jnp.mean(row_grads * row_grads, axis=-1))
    new_rows = rows_table - learn_rate * row_grads / (jnp.sqrt(new_state)[:, None] + epsilon)
    return (new_rows, new_state)

def pack_moves(rows_table, state_rows, counts):
    starts = jnp.cumsum(counts) - counts
    offsets = jnp.arange(CAP, dtype=jnp.int32)
    slot_rows = jnp.clip(starts[:, None] + offsets[None, :], 0, rows_table.shape[0] - 1).astype(jnp.int32)
    live_slots = offsets[None, :] < counts[:, None]
    moved_rows = jnp.where(live_slots[..., None], rows_table[slot_rows], 0.0)
    moved_state = jnp.where(live_slots, state_rows[slot_rows], 0.0)
    return (moved_rows, moved_state)

def reference(table, row_state, bag_ids, bag_lengths, interaction_grad, move_rows):

    def pool_item(packed):
        return pool_table(packed[0], packed[1], packed[2])

    def update_item(packed):
        rows_table, state_rows, bag_rows, bag_len, upstream_rows, counts = packed
        row_grads = row_gradients(rows_table.shape[0], bag_rows, bag_len, upstream_rows)
        new_rows, new_state = adagrad(rows_table, state_rows, row_grads)
        moved_rows, moved_state = pack_moves(new_rows, new_state, counts)
        return (new_rows, new_state, moved_rows, moved_state)

    def one_group(inputs):
        rows_group, state_group, ids_group, len_group, grad_group, move_group = inputs
        pooled = lax.map(pool_item, (rows_group, ids_group, len_group)).astype(jnp.bfloat16)
        symmetric = grad_group + jnp.transpose(grad_group, (1, 0, 2))
        upstream = jnp.einsum('fgb,gbe->fbe', symmetric, pooled.astype(jnp.float32), precision=lax.Precision.HIGHEST).astype(jnp.bfloat16)
        return lax.map(update_item, (rows_group, state_group, ids_group, len_group, upstream, move_group))
    new_table, new_state, moved_rows, moved_state = lax.map(one_group, (table, row_state, bag_ids, bag_lengths, interaction_grad, move_rows))
    arrived = jnp.transpose(moved_rows, (2, 0, 1, 3, 4))
    arrived_state = jnp.transpose(moved_state, (2, 0, 1, 3))
    return (new_table, new_state, arrived, arrived_state)
```

```python
import jax
import jax.numpy as jnp
from jax import lax
from jax.sharding import PartitionSpec as P

CAP = 64


learn_rate = 0.05
epsilon = 1e-08


def three_parts(values):
    high = lax.reduce_precision(values, 8, 7)
    rest = values - high
    middle = lax.reduce_precision(rest, 8, 7)
    low = rest - middle
    return [part.astype(jnp.bfloat16) for part in (high, middle, low)]


def hits(live_ids, num_rows):
    rows = jnp.arange(num_rows, dtype=jnp.int32)
    total = 0.0
    for slot in range(live_ids.shape[0]):
        total = total + jnp.where(live_ids[slot][:, None] == rows[None, :], 1.0, 0.0)
    return total.astype(jnp.bfloat16)


def on_device(table, row_state, bag_ids, bag_lengths, interaction_grad, move_rows):
    rows_table = table[0, 0]
    state_rows = row_state[0, 0]
    bag_rows = bag_ids[0, 0]
    bag_len = bag_lengths[0, 0]
    counts = move_rows[0, 0]
    grad_block = interaction_grad[0]
    shards = lax.axis_size("shard")
    groups = lax.axis_size("group")
    samples = bag_rows.shape[1]
    per_shard = samples // shards
    row_width = rows_table.shape[1]
    num_rows = rows_table.shape[0]
    slots = jnp.arange(bag_rows.shape[0], dtype=jnp.int32)[:, None]
    live_ids = jnp.where(slots < bag_len[None, :], bag_rows, -1)
    hit = hits(live_ids, num_rows)
    pooled = sum(
        jnp.dot(hit, part, preferred_element_type=jnp.float32) for part in three_parts(rows_table)
    ).astype(jnp.bfloat16)
    received = lax.all_to_all(
        pooled.reshape(1, shards, per_shard, row_width),
        "shard",
        split_axis=1,
        concat_axis=0,
        tiled=True,
    )
    received = received.reshape(shards, per_shard, row_width)
    symmetric = grad_block + jnp.transpose(grad_block, (1, 0, 2))
    upstream = jnp.einsum(
        "fgb,gbe->fbe", symmetric, received.astype(jnp.float32), precision=lax.Precision.HIGHEST
    ).astype(jnp.bfloat16)
    returned = lax.all_to_all(
        upstream.reshape(shards, 1, per_shard, row_width),
        "shard",
        split_axis=0,
        concat_axis=1,
        tiled=True,
    )
    returned = returned.reshape(samples, row_width)
    row_grads = lax.dot_general(
        hit, returned, (((0,), (0,)), ((), ())), preferred_element_type=jnp.float32
    )
    new_state = state_rows + jnp.mean(row_grads * row_grads, axis=-1)
    new_rows = rows_table - learn_rate * row_grads / (jnp.sqrt(new_state)[:, None] + epsilon)
    starts = jnp.cumsum(counts) - counts
    offsets = jnp.arange(CAP, dtype=jnp.int32)
    live_slots = offsets[None, :] < counts[:, None]
    scale = jnp.maximum(jnp.max(jnp.abs(new_rows), axis=-1), 1e-30)
    coded = jnp.round(new_rows * (32767.0 / scale)[:, None])
    tail = jnp.zeros((CAP, row_width), jnp.float32)
    padded = jnp.concatenate([coded, tail], axis=0)
    side = jnp.stack([new_state, scale * (1.0 / 32767.0)], axis=0)
    side = jnp.concatenate([side, jnp.zeros((2, CAP), jnp.float32)], axis=1)
    blocks = []
    sides = []
    for group in range(groups):
        block = lax.dynamic_slice_in_dim(padded, starts[group], CAP, axis=0)
        blocks.append(jnp.where(live_slots[group][:, None], block, 0.0).astype(jnp.int16))
        both = lax.dynamic_slice_in_dim(side, starts[group], CAP, axis=1)
        sides.append(jnp.where(live_slots[group][None, :], both, 0.0))
    arrived_code, arrived_side = (
        lax.all_to_all(jnp.stack(blocks), "group", split_axis=0, concat_axis=0, tiled=True),
        lax.all_to_all(jnp.stack(sides), "group", split_axis=0, concat_axis=0, tiled=True),
    )
    arrived = arrived_code.astype(jnp.float32) * arrived_side[:, 1, :, None]
    return (
        new_rows[None, None],
        new_state[None, None],
        arrived.reshape(1, groups, 1, CAP, row_width),
        arrived_side[:, 0].reshape(1, groups, 1, CAP),
    )


def solution(mesh):
    in_specs = (
        P("group", "shard", None, None),
        P("group", "shard", None),
        P("group", "shard", None, None),
        P("group", "shard", None),
        P("group", None, None, "shard"),
        P("group", "shard", None),
    )
    out_specs = (
        P("group", "shard", None, None),
        P("group", "shard", None),
        P("group", None, "shard", None, None),
        P("group", None, "shard", None),
    )
    return jax.shard_map(
        on_device, mesh=mesh, in_specs=in_specs, out_specs=out_specs, check_vma=False
    )
```

```python
import functools

import jax
import jax.numpy as jnp
from jax import lax
from jax.experimental import pallas as pl
from jax.experimental.pallas import tpu as pltpu
from jax.sharding import PartitionSpec as P

MESH = pl.DeviceIdType.MESH
CAP = 64
PARTS = 2
TOP = 32767.0

learn_rate = 0.05
epsilon = 1e-08


def split_three(values):
    high = values.astype(jnp.bfloat16)
    rest = values - high.astype(jnp.float32)
    middle = rest.astype(jnp.bfloat16)
    low = (rest - middle.astype(jnp.float32)).astype(jnp.bfloat16)
    return high, middle, low


def bag_kernel(
    groups, shards, line,
    table_ref, state_ref, ids_ref, len_ref, grad_ref, counts_ref,
    new_table_ref, new_state_ref, code_ref, side_ref,
    ids_col, ids_row, parts, hit, mix, send1, recv1, send2, recv2,
    in_left, in_right, out_left, out_right, grads, state_col, coded, side_col, pick,
    code_send, code_recv, side_send, side_recv, starts,
    send1_sem, recv1_sem, send2_sem, recv2_sem, code_sem, side_sem,
):
    rows, width = table_ref.shape
    slots, samples = ids_ref.shape
    deep = samples // shards // PARTS
    half = width // 2
    part_rows = shards * deep
    lines = shards // line
    group = lax.axis_index("group")
    me = lax.axis_index("shard")
    my_line = me // line
    my_spot = me % line

    wing = groups // 2
    my_wing = group // wing
    my_place = group % wing

    def dest(k):
        return ((my_wing + 1 + k // wing) % 2) * wing + (my_place + k) % wing

    barrier = pltpu.get_barrier_semaphore()

    def greet_shard(k, carry):
        pl.semaphore_signal(
            barrier, inc=1, device_id=(group, (me + k) % shards), device_id_type=MESH
        )
        return carry

    def greet_group(k, carry):
        pl.semaphore_signal(
            barrier, inc=1, device_id=((group + k) % groups, me), device_id_type=MESH
        )
        return carry

    lax.fori_loop(1, shards, greet_shard, 0)
    lax.fori_loop(1, groups, greet_group, 0)

    def block_copy(source, target, send_sem, recv_sem, part, other):
        return pltpu.make_async_remote_copy(
            src_ref=source.at[part, other],
            dst_ref=target.at[part, me],
            send_sem=send_sem.at[part],
            recv_sem=recv_sem.at[part],
            device_id=(group, other),
            device_id_type=MESH,
        )

    def all_blocks(source, target, send_sem, recv_sem, part):
        return pltpu.make_async_remote_copy(
            src_ref=source.at[part, pl.ds(0, shards - 1)],
            dst_ref=target.at[part, pl.ds(0, shards - 1)],
            send_sem=send_sem.at[part],
            recv_sem=recv_sem.at[part],
            device_id=(group, (me + 1) % shards),
            device_id_type=MESH,
        )

    def send_line(source, target, send_sem, recv_sem, part, step):
        first = ((my_line + step) % lines) * line
        for turn in range(line):
            other = first + (my_spot + turn) % line
            copy = block_copy(source, target, send_sem, recv_sem, part, other)
            if turn == 0:
                pl.when(step > 0)(copy.start)
            else:
                copy.start()

    slot = lax.broadcasted_iota(jnp.int32, (slots, samples), 0)
    live = jnp.where(slot < len_ref[...], ids_ref[...], -1)
    live = jnp.concatenate([live, jnp.full((8 - slots, samples), -1, jnp.int32)], axis=0)
    columns = live.T.reshape(shards, PARTS, deep, 8)
    for part in range(PARTS):
        ids_col[part] = columns[:, part]

    high, middle, low = split_three(table_ref[...])
    parts[:, 0:width] = high
    parts[:, width:2 * width] = middle
    parts[:, 2 * width:3 * width] = low

    pl.semaphore_wait(barrier, shards + groups - 2)

    for part in range(PARTS):
        def pool_step(step, carry, part=part):
            first = ((my_line + step) % lines) * line
            column = ids_col[part, pl.ds(first, line)].reshape(line * deep, 8)
            lane = lax.broadcasted_iota(jnp.int32, (line * deep, rows), 1)
            total = jnp.zeros((line * deep, rows), jnp.float32)
            for j in range(slots):
                total = total + jnp.where(column[:, j:j + 1] == lane, 1.0, 0.0)
            product = jnp.dot(
                total.astype(jnp.bfloat16), parts[...], preferred_element_type=jnp.float32
            )
            pooled = product[:, 0:width] + product[:, width:2 * width]
            pooled = pooled + product[:, 2 * width:3 * width]
            send1[part, pl.ds(first, line)] = pooled.astype(jnp.bfloat16).reshape(line, deep, width)
            send_line(send1, recv1, send1_sem, recv1_sem, part, step)
            return carry

        lax.fori_loop(0, lines, pool_step, 0)
        recv1[part, me] = send1[part, me]

    ordered = jnp.concatenate([ids_col[part].reshape(part_rows, 8) for part in range(PARTS)], axis=0)
    ids_row[...] = ordered.T

    def mix_step(b, carry):
        square = grad_ref[pl.ds(b, shards, stride=PARTS * deep), :]
        square = square + square.T
        first, second, third = split_three(square)
        mix[b] = jnp.concatenate([first, second, third], axis=0)
        return carry

    lax.fori_loop(0, PARTS * deep, mix_step, 0)

    row_block = 128 if rows % 128 == 0 else rows

    def hit_step(block, carry):
        base = pl.multiple_of(block * row_block, row_block)
        row = lax.broadcasted_iota(jnp.int32, (row_block, samples), 0) + base
        total = jnp.zeros((row_block, samples), jnp.float32)
        for j in range(slots):
            total = total + jnp.where(ids_row[j:j + 1, :] == row, 1.0, 0.0)
        hit[pl.ds(base, row_block), :] = total.astype(jnp.bfloat16)
        return carry

    lax.fori_loop(0, rows // row_block, hit_step, 0)
    state_col[...] = jnp.broadcast_to(state_ref[...], (128, rows)).T

    acc = jnp.int32(0)
    for h in range(groups):
        starts[h] = acc
        acc = acc + counts_ref[h]

    def pick_step(k, carry):
        other = dest(k)
        place = lax.broadcasted_iota(jnp.int32, (CAP, rows), 0)
        row = lax.broadcasted_iota(jnp.int32, (CAP, rows), 1)
        goal = jnp.where(place < counts_ref[other], place + starts[other], -1)
        pick[k] = jnp.where(goal == row, 1.0, 0.0).astype(jnp.bfloat16)
        return carry

    lax.fori_loop(0, groups, pick_step, 0)

    for part in range(PARTS):
        all_blocks(send1, recv1, send1_sem, recv1_sem, part).wait_recv()
        block = recv1[part].reshape(part_rows, width).astype(jnp.float32)
        in_left[...] = block[:, :half]
        in_right[...] = block[:, half:]

        def sample_step(i, carry, part=part):
            inner = jnp.concatenate(
                [in_left[pl.ds(i, shards, stride=deep), :], in_right[pl.ds(i, shards, stride=deep), :]],
                axis=1,
            ).astype(jnp.bfloat16)
            product = jnp.dot(mix[part * deep + i], inner, preferred_element_type=jnp.float32)
            outer = product[0:shards] + product[shards:2 * shards] + product[2 * shards:3 * shards]
            out_left[pl.ds(i, shards, stride=deep), :] = outer[:, :half]
            out_right[pl.ds(i, shards, stride=deep), :] = outer[:, half:]
            return carry

        lax.fori_loop(0, deep, sample_step, 0)
        both = jnp.concatenate([out_left[...], out_right[...]], axis=1)
        send2[part] = both.astype(jnp.bfloat16).reshape(shards, deep, width)

        def back_step(step, carry, part=part):
            send_line(send2, recv2, send2_sem, recv2_sem, part, step)
            return carry

        lax.fori_loop(0, lines, back_step, 0)
        recv2[part, me] = send2[part, me]

    all_blocks(send2, recv2, send2_sem, recv2_sem, 0).wait_recv()
    grads[...] = jnp.dot(
        hit[:, 0:part_rows], recv2[0].reshape(part_rows, width), preferred_element_type=jnp.float32
    )
    all_blocks(send2, recv2, send2_sem, recv2_sem, 1).wait_recv()

    def update_step(block, carry):
        base = pl.multiple_of(block * row_block, row_block)
        here = pl.ds(base, row_block)
        row_grads = grads[here, :] + jnp.dot(
            hit[here, part_rows:2 * part_rows],
            recv2[1].reshape(part_rows, width),
            preferred_element_type=jnp.float32,
        )
        square = jnp.sum(row_grads * row_grads, axis=-1, keepdims=True) * (1.0 / width)
        new_state = state_col[here, :] + square
        step = learn_rate / (jnp.sqrt(new_state) + epsilon)
        new_rows = table_ref[here, :] - row_grads * step[:, 0:1]
        new_table_ref[here, :] = new_rows
        scale = jnp.maximum(jnp.max(jnp.abs(new_rows), axis=-1, keepdims=True), 1e-30)
        whole = jnp.round(new_rows * (TOP / scale))
        upper = jnp.round(whole * (1.0 / 256.0))
        coded[here, 0:width] = upper.astype(jnp.bfloat16)
        coded[here, width:2 * width] = (whole - upper * 256.0).astype(jnp.bfloat16)
        lane = lax.broadcasted_iota(jnp.int32, (row_block, 128), 1)
        side_col[here, :] = jnp.where(lane == 0, new_state, scale * (1.0 / TOP))
        return carry

    lax.fori_loop(0, rows // row_block, update_step, 0)

    def code_copy(other):
        return pltpu.make_async_remote_copy(
            src_ref=code_send.at[other],
            dst_ref=code_recv.at[group],
            send_sem=code_sem.at[0],
            recv_sem=code_sem.at[1],
            device_id=(other, me),
            device_id_type=MESH,
        )

    def side_copy(other):
        return pltpu.make_async_remote_copy(
            src_ref=side_send.at[other],
            dst_ref=side_recv.at[group],
            send_sem=side_sem.at[0],
            recv_sem=side_sem.at[1],
            device_id=(other, me),
            device_id_type=MESH,
        )

    side_rows = side_col[...].T[0:8]
    side_parts = jnp.concatenate(split_three(side_rows), axis=0)
    band = 4 if groups % 4 == 0 else groups

    def pack_step(block, carry):
        select = pick[pl.ds(block * band, band)].reshape(band * CAP, rows)
        both = jnp.dot(select, coded[...], preferred_element_type=jnp.float32)
        values = both[:, :width] * 256.0 + both[:, width:]
        values = values.astype(jnp.int32).astype(jnp.int16).reshape(band, CAP, width)
        aside = lax.dot_general(
            side_parts, select, (((1,), (1,)), ((), ())), preferred_element_type=jnp.float32
        )
        aside = aside[0:8] + aside[8:16] + aside[16:24]
        for turn in range(band):
            k = block * band + turn
            other = dest(k)
            code_send[other] = values[turn]
            side_send[other, :, 0:CAP] = aside[0:2, turn * CAP:(turn + 1) * CAP]

            @pl.when(k != wing)
            def _():
                code_copy(other).start()
                side_copy(other).start()

        return carry

    side_send[...] = jnp.zeros(side_send.shape, jnp.float32)
    lax.fori_loop(0, groups // band, pack_step, 0)
    code_recv[group] = code_send[group]
    side_recv[group] = side_send[group]

    new_state_ref[...] = side_rows[0:1]

    others = pl.ds(0, groups - 1)
    next_group = (group + 1) % groups
    all_codes = pltpu.make_async_remote_copy(
        src_ref=code_send.at[others],
        dst_ref=code_recv.at[others],
        send_sem=code_sem.at[0],
        recv_sem=code_sem.at[1],
        device_id=(next_group, me),
        device_id_type=MESH,
    )
    all_sides = pltpu.make_async_remote_copy(
        src_ref=side_send.at[others],
        dst_ref=side_recv.at[others],
        send_sem=side_sem.at[0],
        recv_sem=side_sem.at[1],
        device_id=(next_group, me),
        device_id_type=MESH,
    )
    for part in range(PARTS):
        all_blocks(send1, recv1, send1_sem, recv1_sem, part).wait_send()
        all_blocks(send2, recv2, send2_sem, recv2_sem, part).wait_send()
    all_sides.wait_recv()
    side_ref[...] = side_recv[...]
    all_codes.wait_recv()
    code_ref[...] = code_recv[...]
    all_sides.wait_send()
    all_codes.wait_send()


def on_device(table, row_state, bag_ids, bag_lengths, interaction_grad, move_rows):
    groups = lax.axis_size("group")
    shards = lax.axis_size("shard")
    line = 6 if shards % 6 == 0 else 2
    rows, width = table.shape[2:]
    slots, samples = bag_ids.shape[2:]
    deep = samples // shards // PARTS
    squares = jnp.transpose(interaction_grad[0], (0, 2, 1)).reshape(samples, shards)
    in_vmem = pl.BlockSpec(memory_space=pltpu.VMEM)
    in_smem = pl.BlockSpec(memory_space=pltpu.SMEM)
    blocks = (PARTS, shards, deep, width)
    bf16, f32, i32, i16 = jnp.bfloat16, jnp.float32, jnp.int32, jnp.int16
    lanes = (shards * deep, width // 2)
    pair = pltpu.SemaphoreType.DMA((2,))
    new_table, new_state, code, side = pl.pallas_call(
        functools.partial(bag_kernel, groups, shards, line),
        out_shape=(
            jax.ShapeDtypeStruct((rows, width), f32),
            jax.ShapeDtypeStruct((1, rows), f32),
            jax.ShapeDtypeStruct((groups, CAP, width), i16),
            jax.ShapeDtypeStruct((groups, 2, 128), f32),
        ),
        in_specs=[in_vmem] * 5 + [in_smem],
        out_specs=(in_vmem,) * 4,
        scratch_shapes=[
            pltpu.VMEM((PARTS, shards, deep, 8), i32),
            pltpu.VMEM((8, samples), i32),
            pltpu.VMEM((rows, 3 * width), bf16),
            pltpu.VMEM((rows, samples), bf16),
            pltpu.VMEM((PARTS * deep, 3 * shards, shards), bf16),
            pltpu.VMEM(blocks, bf16),
            pltpu.VMEM(blocks, bf16),
            pltpu.VMEM(blocks, bf16),
            pltpu.VMEM(blocks, bf16),
            pltpu.VMEM(lanes, f32),
            pltpu.VMEM(lanes, f32),
            pltpu.VMEM(lanes, f32),
            pltpu.VMEM(lanes, f32),
            pltpu.VMEM((rows, width), f32),
            pltpu.VMEM((rows, 128), f32),
            pltpu.VMEM((rows, 2 * width), bf16),
            pltpu.VMEM((rows, 128), f32),
            pltpu.VMEM((groups, CAP, rows), bf16),
            pltpu.VMEM((groups, CAP, width), i16),
            pltpu.VMEM((groups, CAP, width), i16),
            pltpu.VMEM((groups, 2, 128), f32),
            pltpu.VMEM((groups, 2, 128), f32),
            pltpu.SMEM((groups,), i32),
            pair, pair, pair, pair, pair, pair,
        ],
        compiler_params=pltpu.CompilerParams(
            collective_id=0, has_side_effects=True, vmem_limit_bytes=48 * 1024 * 1024
        ),
        cost_estimate=pl.CostEstimate(
            flops=8 * samples * rows * width, bytes_accessed=6 * rows * width * 4, transcendentals=0
        ),
    )(
        table[0, 0],
        row_state[0],
        bag_ids[0, 0],
        bag_lengths[0],
        squares,
        move_rows[0, 0],
    )
    arrived = code.astype(jnp.float32) * side[:, 1, :CAP, None]
    return (
        new_table[None, None],
        new_state[None],
        arrived.reshape(1, groups, 1, CAP, width),
        side[:, 0, :CAP].reshape(1, groups, 1, CAP),
    )


def solution(mesh):
    in_specs = (
        P("group", "shard", None, None),
        P("group", "shard", None),
        P("group", "shard", None, None),
        P("group", "shard", None),
        P("group", None, None, "shard"),
        P("group", "shard", None),
    )
    out_specs = (
        P("group", "shard", None, None),
        P("group", "shard", None),
        P("group", None, "shard", None, None),
        P("group", None, "shard", None),
    )
    return jax.shard_map(
        on_device, mesh=mesh, in_specs=in_specs, out_specs=out_specs, check_vma=False
    )
```

```python
import functools

import jax
import jax.numpy as jnp
from jax import lax
from jax.experimental import pallas as pl
from jax.experimental.pallas import tpu as pltpu
from jax.sharding import PartitionSpec as P

MESH = pl.DeviceIdType.MESH
CAP = 64
PARTS = 2
TOP = 32767.0
VMEM_BYTES = 60 * 1024 * 1024

learn_rate = 0.05
epsilon = 1e-08


def split_three(values):
    high = values.astype(jnp.bfloat16)
    rest = values - high.astype(jnp.float32)
    middle = rest.astype(jnp.bfloat16)
    low = (rest - middle.astype(jnp.float32)).astype(jnp.bfloat16)
    return high, middle, low


def bag_kernel(
    groups, shards, line,
    table_hbm, state_hbm, ids_hbm, len_hbm, grad_hbm, counts_hbm,
    new_table_hbm, new_state_hbm, code_recv, side_recv,
    table_ref, state_ref, ids_ref, len_ref, grad_ref, counts_ref,
    ids_col, ids_row, parts, state_parts, hit, picked_hit, mix, send1, recv1, send2, recv2,
    in_left, in_right, out_left, out_right, grads, picked_grads, picked_table, picked_state,
    state_col, new_col, new_table_ref, new_state_ref, code_send, side_send, starts,
    load_sem, store_sem, send1_sem, recv1_sem, send2_sem, recv2_sem, code_sem, side_sem,
):
    rows, width = table_ref.shape
    slots, samples = ids_ref.shape
    deep = samples // shards // PARTS
    half = width // 2
    part_rows = shards * deep
    lines = shards // line
    group = lax.axis_index("group")
    me = lax.axis_index("shard")
    my_line = me // line
    my_spot = me % line
    wing = groups // 2
    my_wing = group // wing
    my_place = group % wing

    loads = [
        pltpu.make_async_copy(source, target, load_sem.at[i])
        for i, (source, target) in enumerate((
            (ids_hbm, ids_ref),
            (len_hbm, len_ref),
            (table_hbm, table_ref),
            (grad_hbm, grad_ref),
            (state_hbm, state_ref),
            (counts_hbm, counts_ref),
        ))
    ]
    for load in loads:
        load.start()

    def dest(k):
        return ((my_wing + 1 + k // wing) % 2) * wing + (my_place + k) % wing

    barrier = pltpu.get_barrier_semaphore()

    def greet_shard(k, carry):
        pl.semaphore_signal(
            barrier, inc=1, device_id=(group, (me + k) % shards), device_id_type=MESH
        )
        return carry

    def greet_group(k, carry):
        pl.semaphore_signal(
            barrier, inc=1, device_id=((group + k) % groups, me), device_id_type=MESH
        )
        return carry

    lax.fori_loop(1, shards, greet_shard, 0)
    lax.fori_loop(1, groups, greet_group, 0)

    def block_copy(source, target, send_sem, recv_sem, part, other):
        return pltpu.make_async_remote_copy(
            src_ref=source.at[part, other],
            dst_ref=target.at[part, me],
            send_sem=send_sem.at[part],
            recv_sem=recv_sem.at[part],
            device_id=(group, other),
            device_id_type=MESH,
        )

    def all_blocks(source, target, send_sem, recv_sem, part):
        return pltpu.make_async_remote_copy(
            src_ref=source.at[part, pl.ds(0, shards - 1)],
            dst_ref=target.at[part, pl.ds(0, shards - 1)],
            send_sem=send_sem.at[part],
            recv_sem=recv_sem.at[part],
            device_id=(group, (me + 1) % shards),
            device_id_type=MESH,
        )

    def send_line(source, target, send_sem, recv_sem, part, step, first_turn):
        first = ((my_line + step) % lines) * line
        for turn in range(first_turn, line):
            other = first + (my_spot + turn) % line
            block_copy(source, target, send_sem, recv_sem, part, other).start()

    loads[0].wait()
    loads[1].wait()
    slot = lax.broadcasted_iota(jnp.int32, (slots, samples), 0)
    live = jnp.where(slot < len_ref[...], ids_ref[...], -1)
    live = jnp.concatenate([live, jnp.full((8 - slots, samples), -1, jnp.int32)], axis=0)
    columns = live.T.reshape(shards, PARTS, deep, 8)
    for part in range(PARTS):
        ids_col[part] = columns[:, part]

    loads[2].wait()
    high, middle, low = split_three(table_ref[...])
    parts[:, 0:width] = high
    parts[:, width:2 * width] = middle
    parts[:, 2 * width:3 * width] = low

    def pool_line(part, step):
        first = ((my_line + step) % lines) * line
        column = ids_col[part, pl.ds(first, line)].reshape(line * deep, 8)
        lane = lax.broadcasted_iota(jnp.int32, (line * deep, rows), 1)
        total = jnp.zeros((line * deep, rows), jnp.float32)
        for j in range(slots):
            total = total + jnp.where(column[:, j:j + 1] == lane, 1.0, 0.0)
        product = jnp.dot(
            total.astype(jnp.bfloat16), parts[...], preferred_element_type=jnp.float32
        )
        pooled = product[:, 0:width] + product[:, width:2 * width]
        pooled = pooled + product[:, 2 * width:3 * width]
        send1[part, pl.ds(first, line)] = pooled.astype(jnp.bfloat16).reshape(line, deep, width)

    for part in range(PARTS):
        def pool_step(step, carry, part=part):
            pool_line(part, step)
            send_line(send1, recv1, send1_sem, recv1_sem, part, step, 0)
            return carry

        pool_line(part, 0)
        if part == 0:
            pl.semaphore_wait(barrier, shards + groups - 2)
        send_line(send1, recv1, send1_sem, recv1_sem, part, 0, 1)
        lax.fori_loop(1, lines, pool_step, 0)
        recv1[part, me] = send1[part, me]

    loads[3].wait()

    def mix_step(b, carry):
        square = grad_ref[pl.ds(b, shards, stride=PARTS * deep), :]
        square = square + square.T
        first, second, third = split_three(square)
        mix[b] = jnp.concatenate([first, second, third], axis=0)
        return carry

    lax.fori_loop(0, PARTS * deep, mix_step, 0)

    def mix_part(part):
        all_blocks(send1, recv1, send1_sem, recv1_sem, part).wait_recv()
        block = recv1[part].reshape(part_rows, width).astype(jnp.float32)
        in_left[...] = block[:, :half]
        in_right[...] = block[:, half:]

        def sample_step(i, carry):
            inner = jnp.concatenate(
                [in_left[pl.ds(i, shards, stride=deep), :], in_right[pl.ds(i, shards, stride=deep), :]],
                axis=1,
            ).astype(jnp.bfloat16)
            product = jnp.dot(mix[part * deep + i], inner, preferred_element_type=jnp.float32)
            outer = product[0:shards] + product[shards:2 * shards] + product[2 * shards:3 * shards]
            out_left[pl.ds(i, shards, stride=deep), :] = outer[:, :half]
            out_right[pl.ds(i, shards, stride=deep), :] = outer[:, half:]
            return carry

        lax.fori_loop(0, deep, sample_step, 0)
        both = jnp.concatenate([out_left[...], out_right[...]], axis=1)
        send2[part] = both.astype(jnp.bfloat16).reshape(shards, deep, width)

        def back_step(step, carry):
            send_line(send2, recv2, send2_sem, recv2_sem, part, step, 0)
            return carry

        send_line(send2, recv2, send2_sem, recv2_sem, part, 0, 1)
        lax.fori_loop(1, lines, back_step, 0)
        recv2[part, me] = send2[part, me]

    mix_part(0)

    ordered = jnp.concatenate([ids_col[part].reshape(part_rows, 8) for part in range(PARTS)], axis=0)
    ids_row[...] = ordered.T
    loads[4].wait()
    loads[5].wait()
    state_col[...] = jnp.broadcast_to(state_ref[...], (128, rows)).T
    acc = jnp.int32(0)
    for h in range(groups):
        starts[h] = acc
        acc = acc + counts_ref[0, h]
    lane = lax.broadcasted_iota(jnp.int32, (rows, 128), 1)
    first, second, third = (piece.astype(jnp.float32) for piece in split_three(state_col[...]))
    state_parts[...] = jnp.where(
        lane == 0, first, jnp.where(lane == 1, second, jnp.where(lane == 2, third, 0.0))
    ).astype(jnp.bfloat16)

    band = 4 if groups % 4 == 0 else groups
    tall = band * CAP

    def goals(block):
        place = lax.broadcasted_iota(jnp.int32, (CAP, 128), 0)
        pieces = []
        for turn in range(band):
            other = dest(block * band + turn)
            pieces.append(jnp.where(place < counts_ref[0, other], place + starts[other], -2))
        return jnp.concatenate(pieces, axis=0)[:, 0:1]

    def count_hits(goal, size):
        total = jnp.zeros((size, samples), jnp.float32)
        for j in range(slots):
            total = total + jnp.where(ids_row[j:j + 1, :] == goal, 1.0, 0.0)
        return total.astype(jnp.bfloat16)

    def pick_step(block, carry):
        here = pl.ds(pl.multiple_of(block * tall, tall), tall)
        goal = goals(block)
        for piece in range(2):
            span = slice(piece * tall // 2, (piece + 1) * tall // 2)
            at = pl.ds(pl.multiple_of(block * tall + piece * tall // 2, tall // 2), tall // 2)
            picked_hit[at, :] = count_hits(goal[span], tall // 2)
        pick = jnp.where(
            goal == lax.broadcasted_iota(jnp.int32, (tall, rows), 1), 1.0, 0.0
        ).astype(jnp.bfloat16)
        product = jnp.dot(pick, parts[...], preferred_element_type=jnp.float32)
        both = product[:, 0:width] + product[:, width:2 * width]
        picked_table[here, :] = both + product[:, 2 * width:3 * width]
        product = jnp.dot(pick, state_parts[...], preferred_element_type=jnp.float32)
        total = (product[:, 0:1] + product[:, 1:2]) + product[:, 2:3]
        picked_state[here, :] = jnp.broadcast_to(total, (tall, 128))
        return carry

    lax.fori_loop(0, groups // band, pick_step, 0)

    mix_part(1)

    row_block = 128 if rows % 128 == 0 else rows

    def hit_step(block, carry):
        base = pl.multiple_of(block * row_block, row_block)
        row = lax.broadcasted_iota(jnp.int32, (row_block, samples), 0) + base
        hit[pl.ds(base, row_block), :] = count_hits(row, row_block)
        return carry

    lax.fori_loop(0, rows // row_block, hit_step, 0)
    side_send[...] = jnp.zeros(side_send.shape, jnp.float32)

    all_blocks(send2, recv2, send2_sem, recv2_sem, 0).wait_recv()
    returned = recv2[0].reshape(part_rows, width)
    picked_grads[...] = jnp.dot(
        picked_hit[:, 0:part_rows], returned, preferred_element_type=jnp.float32
    )
    grads[...] = jnp.dot(hit[:, 0:part_rows], returned, preferred_element_type=jnp.float32)

    def adagrad(old_rows, old_state, row_grads):
        square = jnp.sum(row_grads * row_grads, axis=-1, keepdims=True) * (1.0 / width)
        new_state = old_state + square
        step = learn_rate / (jnp.sqrt(new_state) + epsilon)
        return old_rows - row_grads * step[:, 0:1], new_state

    def code_copy(other):
        return pltpu.make_async_remote_copy(
            src_ref=code_send.at[other],
            dst_ref=code_recv.at[group],
            send_sem=code_sem.at[0],
            recv_sem=code_sem.at[1],
            device_id=(other, me),
            device_id_type=MESH,
        )

    def side_copy(other):
        return pltpu.make_async_remote_copy(
            src_ref=side_send.at[other],
            dst_ref=side_recv.at[group],
            send_sem=side_sem.at[0],
            recv_sem=side_sem.at[1],
            device_id=(other, me),
            device_id_type=MESH,
        )

    all_blocks(send2, recv2, send2_sem, recv2_sem, 1).wait_recv()

    def pack_step(block, carry):
        here = pl.ds(pl.multiple_of(block * tall, tall), tall)
        row_grads = picked_grads[here, :] + jnp.dot(
            picked_hit[here, part_rows:2 * part_rows],
            recv2[1].reshape(part_rows, width),
            preferred_element_type=jnp.float32,
        )
        new_rows, new_state = adagrad(picked_table[here, :], picked_state[here, :], row_grads)
        scale = jnp.maximum(jnp.max(jnp.abs(new_rows), axis=-1, keepdims=True), 1e-30)
        values = jnp.round(new_rows * (TOP / scale))
        values = values.astype(jnp.int32).astype(jnp.int16).reshape(band, CAP, width)
        at = lax.broadcasted_iota(jnp.int32, (tall, 128), 1)
        aside = jnp.where(at == 0, new_state, scale * (1.0 / TOP)).T
        for turn in range(band):
            k = block * band + turn
            other = dest(k)
            code_send[other] = values[turn]
            side_send[other, :, 0:CAP] = aside[0:2, turn * CAP:(turn + 1) * CAP]

            @pl.when(k != wing)
            def _():
                code_copy(other).start()
                side_copy(other).start()

        return carry

    lax.fori_loop(0, groups // band, pack_step, 0)
    stores = [
        pltpu.make_async_copy(source, target, store_sem.at[i])
        for i, (source, target) in enumerate((
            (code_send.at[group], code_recv.at[group]),
            (side_send.at[group], side_recv.at[group]),
            (new_table_ref, new_table_hbm),
            (new_state_ref, new_state_hbm),
        ))
    ]
    stores[0].start()
    stores[1].start()

    def update_step(block, carry):
        base = pl.multiple_of(block * row_block, row_block)
        here = pl.ds(base, row_block)
        row_grads = grads[here, :] + jnp.dot(
            hit[here, part_rows:2 * part_rows],
            recv2[1].reshape(part_rows, width),
            preferred_element_type=jnp.float32,
        )
        new_rows, new_state = adagrad(table_ref[here, :], state_col[here, :], row_grads)
        new_table_ref[here, :] = new_rows
        new_col[here, :] = new_state
        return carry

    lax.fori_loop(0, rows // row_block, update_step, 0)
    stores[2].start()
    new_state_ref[...] = new_col[...].T[0:1]
    stores[3].start()

    others = pl.ds(0, groups - 1)
    next_group = (group + 1) % groups
    all_codes = pltpu.make_async_remote_copy(
        src_ref=code_send.at[others],
        dst_ref=code_recv.at[others],
        send_sem=code_sem.at[0],
        recv_sem=code_sem.at[1],
        device_id=(next_group, me),
        device_id_type=MESH,
    )
    all_sides = pltpu.make_async_remote_copy(
        src_ref=side_send.at[others],
        dst_ref=side_recv.at[others],
        send_sem=side_sem.at[0],
        recv_sem=side_sem.at[1],
        device_id=(next_group, me),
        device_id_type=MESH,
    )
    for part in range(PARTS):
        all_blocks(send1, recv1, send1_sem, recv1_sem, part).wait_send()
        all_blocks(send2, recv2, send2_sem, recv2_sem, part).wait_send()
    for store in stores:
        store.wait()
    all_sides.wait_send()
    all_codes.wait_send()
    all_sides.wait_recv()
    all_codes.wait_recv()


def finish_kernel(
    table_hbm, state_hbm, code_hbm, side_hbm,
    new_table_ref, new_state_ref, arrived_ref, arrived_state_ref,
    code_ref, side_ref, decoded, states, in_sems, out_sems,
):
    groups = code_ref.shape[0]
    pieces = 4
    band = groups // pieces
    side_in = pltpu.make_async_copy(side_hbm, side_ref, in_sems.at[0])
    side_in.start()
    codes_in = []
    for block in range(pieces):
        here = pl.ds(block * band, band)
        copy = pltpu.make_async_copy(code_hbm.at[here], code_ref.at[here], in_sems.at[1 + block])
        copy.start()
        codes_in.append(copy)
    copies = [
        pltpu.make_async_copy(table_hbm, new_table_ref.at[0, 0], out_sems.at[0]),
        pltpu.make_async_copy(state_hbm, new_state_ref.at[0], out_sems.at[1]),
        pltpu.make_async_copy(states, arrived_state_ref, out_sems.at[2]),
    ]
    copies[0].start()
    copies[1].start()
    side_in.wait()
    states[0] = side_ref[:, 0:1, 0:CAP]
    copies[2].start()
    scales = side_ref[:, 1, :].T
    for block in range(pieces):
        codes_in[block].wait()
        for turn in range(band):
            h = block * band + turn
            decoded[0, h, 0] = code_ref[h].astype(jnp.float32) * scales[0:CAP, h:h + 1]
        here = pl.ds(block * band, band)
        copy = pltpu.make_async_copy(
            decoded.at[0, here], arrived_ref.at[0, here], out_sems.at[3 + block]
        )
        copy.start()
        copies.append(copy)
    for copy in copies:
        copy.wait()


def on_device(table, row_state, bag_ids, bag_lengths, interaction_grad, move_rows):
    groups = lax.axis_size("group")
    shards = lax.axis_size("shard")
    line = 6 if shards % 6 == 0 else 2
    rows, width = table.shape[2:]
    slots, samples = bag_ids.shape[2:]
    deep = samples // shards // PARTS
    squares = jnp.transpose(interaction_grad[0], (0, 2, 1)).reshape(samples, shards)
    in_hbm = pl.BlockSpec(memory_space=pltpu.HBM)
    blocks = (PARTS, shards, deep, width)
    bf16, f32, i32, i16 = jnp.bfloat16, jnp.float32, jnp.int32, jnp.int16
    lanes = (shards * deep, width // 2)
    moved = groups * CAP
    pair = pltpu.SemaphoreType.DMA((2,))
    new_table, new_state, code, side = pl.pallas_call(
        functools.partial(bag_kernel, groups, shards, line),
        name="bags",
        out_shape=(
            jax.ShapeDtypeStruct((rows, width), f32),
            jax.ShapeDtypeStruct((1, rows), f32),
            jax.ShapeDtypeStruct((groups, CAP, width), i16),
            jax.ShapeDtypeStruct((groups, 2, 128), f32),
        ),
        in_specs=[in_hbm] * 6,
        out_specs=(in_hbm,) * 4,
        scratch_shapes=[
            pltpu.VMEM((rows, width), f32),
            pltpu.VMEM((1, rows), f32),
            pltpu.VMEM((slots, samples), i32),
            pltpu.VMEM((1, samples), i32),
            pltpu.VMEM((samples, shards), f32),
            pltpu.SMEM((1, groups), i32),
            pltpu.VMEM((PARTS, shards, deep, 8), i32),
            pltpu.VMEM((8, samples), i32),
            pltpu.VMEM((rows, 3 * width), bf16),
            pltpu.VMEM((rows, 128), bf16),
            pltpu.VMEM((rows, samples), bf16),
            pltpu.VMEM((moved, samples), bf16),
            pltpu.VMEM((PARTS * deep, 3 * shards, shards), bf16),
            pltpu.VMEM(blocks, bf16),
            pltpu.VMEM(blocks, bf16),
            pltpu.VMEM(blocks, bf16),
            pltpu.VMEM(blocks, bf16),
            pltpu.VMEM(lanes, f32),
            pltpu.VMEM(lanes, f32),
            pltpu.VMEM(lanes, f32),
            pltpu.VMEM(lanes, f32),
            pltpu.VMEM((rows, width), f32),
            pltpu.VMEM((moved, width), f32),
            pltpu.VMEM((moved, width), f32),
            pltpu.VMEM((moved, 128), f32),
            pltpu.VMEM((rows, 128), f32),
            pltpu.VMEM((rows, 128), f32),
            pltpu.VMEM((rows, width), f32),
            pltpu.VMEM((1, rows), f32),
            pltpu.VMEM((groups, CAP, width), i16),
            pltpu.VMEM((groups, 2, 128), f32),
            pltpu.SMEM((groups,), i32),
            pltpu.SemaphoreType.DMA((6,)),
            pltpu.SemaphoreType.DMA((4,)),
            pair, pair, pair, pair, pair, pair,
        ],
        compiler_params=pltpu.CompilerParams(
            collective_id=0, has_side_effects=True, vmem_limit_bytes=VMEM_BYTES
        ),
        cost_estimate=pl.CostEstimate(
            flops=12 * samples * rows * width, bytes_accessed=6 * rows * width * 4, transcendentals=0
        ),
    )(
        table[0, 0],
        row_state[0],
        bag_ids[0, 0],
        bag_lengths[0],
        squares,
        move_rows[0],
    )
    return pl.pallas_call(
        finish_kernel,
        name="finish",
        out_shape=(
            jax.ShapeDtypeStruct((1, 1, rows, width), f32),
            jax.ShapeDtypeStruct((1, 1, rows), f32),
            jax.ShapeDtypeStruct((1, groups, 1, CAP, width), f32),
            jax.ShapeDtypeStruct((1, groups, 1, CAP), f32),
        ),
        in_specs=[in_hbm] * 4,
        out_specs=(in_hbm,) * 4,
        scratch_shapes=[
            pltpu.VMEM((groups, CAP, width), i16),
            pltpu.VMEM((groups, 2, 128), f32),
            pltpu.VMEM((1, groups, 1, CAP, width), f32),
            pltpu.VMEM((1, groups, 1, CAP), f32),
            pltpu.SemaphoreType.DMA((5,)),
            pltpu.SemaphoreType.DMA((7,)),
        ],
        compiler_params=pltpu.CompilerParams(vmem_limit_bytes=VMEM_BYTES),
        cost_estimate=pl.CostEstimate(
            flops=rows * width, bytes_accessed=10 * rows * width, transcendentals=0
        ),
    )(new_table, new_state, code, side)


def solution(mesh):
    in_specs = (
        P("group", "shard", None, None),
        P("group", "shard", None),
        P("group", "shard", None, None),
        P("group", "shard", None),
        P("group", None, None, "shard"),
        P("group", "shard", None),
    )
    out_specs = (
        P("group", "shard", None, None),
        P("group", "shard", None),
        P("group", None, "shard", None, None),
        P("group", None, "shard", None),
    )
    return jax.shard_map(
        on_device, mesh=mesh, in_specs=in_specs, out_specs=out_specs, check_vma=False
    )
```

```python
import functools

import jax
import jax.numpy as jnp
from jax import lax
from jax.experimental import pallas as pl
from jax.experimental.pallas import tpu as pltpu
from jax.sharding import PartitionSpec as P

MESH = pl.DeviceIdType.MESH
CAP = 64
PARTS = 2
TOP = 32767.0
VMEM_BYTES = 60 * 1024 * 1024

learn_rate = 0.05
epsilon = 1e-08


def split_three(values):
    high = values.astype(jnp.bfloat16)
    rest = values - high.astype(jnp.float32)
    middle = rest.astype(jnp.bfloat16)
    low = (rest - middle.astype(jnp.float32)).astype(jnp.bfloat16)
    return high, middle, low


def bag_kernel(
    groups, shards, line,
    table_hbm, state_hbm, ids_hbm, len_hbm, grad_hbm, counts_hbm,
    new_table_hbm, new_state_hbm, code_recv, side_recv,
    table_ref, state_ref, ids_ref, len_ref, grad_ref, counts_ref,
    ids_col, ids_row, parts, state_parts, hit, picked_hit, mix, send1, recv1, send2, recv2,
    in_left, in_right, out_left, out_right, grads, picked_grads, picked_table, picked_state,
    state_col, new_col, new_table_ref, new_state_ref, code_send, side_send, starts,
    load_sem, store_sem, send1_sem, recv1_sem, send2_sem, recv2_sem, code_sem, side_sem,
):
    rows, width = table_ref.shape
    slots, samples = ids_ref.shape
    deep = samples // shards // PARTS
    half = width // 2
    part_rows = shards * deep
    lines = shards // line
    group = lax.axis_index("group")
    me = lax.axis_index("shard")
    my_line = me // line
    my_spot = me % line
    wing = groups // 2
    my_wing = group // wing
    my_place = group % wing

    loads = [
        pltpu.make_async_copy(source, target, load_sem.at[i])
        for i, (source, target) in enumerate((
            (ids_hbm, ids_ref),
            (len_hbm, len_ref),
            (table_hbm, table_ref),
            (grad_hbm, grad_ref),
            (state_hbm, state_ref),
            (counts_hbm, counts_ref),
        ))
    ]
    for load in loads:
        load.start()

    def dest(k):
        return ((my_wing + 1 + k // wing) % 2) * wing + (my_place + k) % wing

    barrier = pltpu.get_barrier_semaphore()

    def greet_shard(k, carry):
        pl.semaphore_signal(
            barrier, inc=1, device_id=(group, (me + k) % shards), device_id_type=MESH
        )
        return carry

    def greet_group(k, carry):
        pl.semaphore_signal(
            barrier, inc=1, device_id=((group + k) % groups, me), device_id_type=MESH
        )
        return carry

    lax.fori_loop(1, shards, greet_shard, 0)
    lax.fori_loop(1, groups, greet_group, 0)

    def block_copy(source, target, send_sem, recv_sem, part, other):
        return pltpu.make_async_remote_copy(
            src_ref=source.at[part, other],
            dst_ref=target.at[part, me],
            send_sem=send_sem.at[part],
            recv_sem=recv_sem.at[part],
            device_id=(group, other),
            device_id_type=MESH,
        )

    def all_blocks(source, target, send_sem, recv_sem, part):
        return pltpu.make_async_remote_copy(
            src_ref=source.at[part, pl.ds(0, shards - 1)],
            dst_ref=target.at[part, pl.ds(0, shards - 1)],
            send_sem=send_sem.at[part],
            recv_sem=recv_sem.at[part],
            device_id=(group, (me + 1) % shards),
            device_id_type=MESH,
        )

    def send_line(source, target, send_sem, recv_sem, part, step, first_turn):
        first = ((my_line + step) % lines) * line
        for turn in range(first_turn, line):
            other = first + (my_spot + turn) % line
            block_copy(source, target, send_sem, recv_sem, part, other).start()

    loads[0].wait()
    loads[1].wait()
    slot = lax.broadcasted_iota(jnp.int32, (slots, samples), 0)
    live = jnp.where(slot < len_ref[...], ids_ref[...], -1)
    live = jnp.concatenate([live, jnp.full((8 - slots, samples), -1, jnp.int32)], axis=0)
    columns = live.T.reshape(shards, PARTS, deep, 8)
    for part in range(PARTS):
        ids_col[part] = columns[:, part]

    loads[2].wait()
    high, middle, low = split_three(table_ref[...])
    parts[:, 0:width] = high
    parts[:, width:2 * width] = middle
    parts[:, 2 * width:3 * width] = low

    def pool_line(part, step):
        first = ((my_line + step) % lines) * line
        column = ids_col[part, pl.ds(first, line)].reshape(line * deep, 8)
        lane = lax.broadcasted_iota(jnp.int32, (line * deep, rows), 1)
        total = jnp.zeros((line * deep, rows), jnp.float32)
        for j in range(slots):
            total = total + jnp.where(column[:, j:j + 1] == lane, 1.0, 0.0)
        product = jnp.dot(
            total.astype(jnp.bfloat16), parts[...], preferred_element_type=jnp.float32
        )
        pooled = product[:, 0:width] + product[:, width:2 * width]
        pooled = pooled + product[:, 2 * width:3 * width]
        send1[part, pl.ds(first, line)] = pooled.astype(jnp.bfloat16).reshape(line, deep, width)

    for part in range(PARTS):
        def pool_step(step, carry, part=part):
            pool_line(part, step)
            send_line(send1, recv1, send1_sem, recv1_sem, part, step, 0)
            return carry

        pool_line(part, 0)
        if part == 0:
            pl.semaphore_wait(barrier, shards + groups - 2)
        send_line(send1, recv1, send1_sem, recv1_sem, part, 0, 1)
        lax.fori_loop(1, lines, pool_step, 0)
        recv1[part, me] = send1[part, me]

    loads[3].wait()

    def mix_step(b, carry):
        square = grad_ref[pl.ds(b, shards, stride=PARTS * deep), :]
        square = square + square.T
        first, second, third = split_three(square)
        mix[b] = jnp.concatenate([first, second, third], axis=0)
        return carry

    lax.fori_loop(0, PARTS * deep, mix_step, 0)

    def mix_part(part):
        all_blocks(send1, recv1, send1_sem, recv1_sem, part).wait_recv()
        block = recv1[part].reshape(part_rows, width).astype(jnp.float32)
        in_left[...] = block[:, :half]
        in_right[...] = block[:, half:]

        def sample_step(i, carry):
            inner = jnp.concatenate(
                [in_left[pl.ds(i, shards, stride=deep), :], in_right[pl.ds(i, shards, stride=deep), :]],
                axis=1,
            ).astype(jnp.bfloat16)
            product = jnp.dot(mix[part * deep + i], inner, preferred_element_type=jnp.float32)
            outer = product[0:shards] + product[shards:2 * shards] + product[2 * shards:3 * shards]
            out_left[pl.ds(i, shards, stride=deep), :] = outer[:, :half]
            out_right[pl.ds(i, shards, stride=deep), :] = outer[:, half:]
            return carry

        lax.fori_loop(0, deep, sample_step, 0)
        both = jnp.concatenate([out_left[...], out_right[...]], axis=1)
        send2[part] = both.astype(jnp.bfloat16).reshape(shards, deep, width)

        def back_step(step, carry):
            if part == 0:
                send_line(send2, recv2, send2_sem, recv2_sem, part, step, 0)
                return carry
            odd = step // lines
            first = ((my_line + step) % lines) * line
            for turn in range(line // 2):
                other = first + ((my_spot // 2 + turn) % (line // 2)) * 2 + odd
                copy = block_copy(send2, recv2, send2_sem, recv2_sem, part, other)
                if turn == 0:
                    pl.when(other != me)(copy.start)
                else:
                    copy.start()
            return carry

        if part == 0:
            send_line(send2, recv2, send2_sem, recv2_sem, part, 0, 1)
            lax.fori_loop(1, lines, back_step, 0)
        else:
            lax.fori_loop(0, 2 * lines, back_step, 0)
        recv2[part, me] = send2[part, me]

    mix_part(0)

    ordered = jnp.concatenate([ids_col[part].reshape(part_rows, 8) for part in range(PARTS)], axis=0)
    ids_row[...] = ordered.T
    loads[4].wait()
    loads[5].wait()
    state_col[...] = jnp.broadcast_to(state_ref[...], (128, rows)).T
    acc = jnp.int32(0)
    for h in range(groups):
        starts[h] = acc
        acc = acc + counts_ref[0, h]
    lane = lax.broadcasted_iota(jnp.int32, (rows, 128), 1)
    first, second, third = (piece.astype(jnp.float32) for piece in split_three(state_col[...]))
    state_parts[...] = jnp.where(
        lane == 0, first, jnp.where(lane == 1, second, jnp.where(lane == 2, third, 0.0))
    ).astype(jnp.bfloat16)

    band = 4 if groups % 4 == 0 else groups
    tall = band * CAP

    def goals(block):
        place = lax.broadcasted_iota(jnp.int32, (CAP, 128), 0)
        pieces = []
        for turn in range(band):
            other = dest(block * band + turn)
            pieces.append(jnp.where(place < counts_ref[0, other], place + starts[other], -2))
        return jnp.concatenate(pieces, axis=0)[:, 0:1]

    def count_hits(goal, size):
        total = jnp.zeros((size, samples), jnp.float32)
        for j in range(slots):
            total = total + jnp.where(ids_row[j:j + 1, :] == goal, 1.0, 0.0)
        return total.astype(jnp.bfloat16)

    def pick_step(block, carry):
        here = pl.ds(pl.multiple_of(block * tall, tall), tall)
        goal = goals(block)
        for piece in range(2):
            span = slice(piece * tall // 2, (piece + 1) * tall // 2)
            at = pl.ds(pl.multiple_of(block * tall + piece * tall // 2, tall // 2), tall // 2)
            picked_hit[at, :] = count_hits(goal[span], tall // 2)
        pick = jnp.where(
            goal == lax.broadcasted_iota(jnp.int32, (tall, rows), 1), 1.0, 0.0
        ).astype(jnp.bfloat16)
        product = jnp.dot(pick, parts[...], preferred_element_type=jnp.float32)
        both = product[:, 0:width] + product[:, width:2 * width]
        picked_table[here, :] = both + product[:, 2 * width:3 * width]
        product = jnp.dot(pick, state_parts[...], preferred_element_type=jnp.float32)
        total = (product[:, 0:1] + product[:, 1:2]) + product[:, 2:3]
        picked_state[here, :] = jnp.broadcast_to(total, (tall, 128))
        return carry

    lax.fori_loop(0, groups // band, pick_step, 0)

    mix_part(1)

    row_block = 128 if rows % 128 == 0 else rows

    def hit_step(block, carry):
        base = pl.multiple_of(block * row_block, row_block)
        row = lax.broadcasted_iota(jnp.int32, (row_block, samples), 0) + base
        hit[pl.ds(base, row_block), :] = count_hits(row, row_block)
        return carry

    lax.fori_loop(0, rows // row_block, hit_step, 0)
    side_send[...] = jnp.zeros(side_send.shape, jnp.float32)

    all_blocks(send2, recv2, send2_sem, recv2_sem, 0).wait_recv()
    returned = recv2[0].reshape(part_rows, width)
    picked_grads[...] = jnp.dot(
        picked_hit[:, 0:part_rows], returned, preferred_element_type=jnp.float32
    )
    grads[...] = jnp.dot(hit[:, 0:part_rows], returned, preferred_element_type=jnp.float32)

    def adagrad(old_rows, old_state, row_grads):
        square = jnp.sum(row_grads * row_grads, axis=-1, keepdims=True) * (1.0 / width)
        new_state = old_state + square
        step = learn_rate / (jnp.sqrt(new_state) + epsilon)
        return old_rows - row_grads * step[:, 0:1], new_state

    def code_copy(other):
        return pltpu.make_async_remote_copy(
            src_ref=code_send.at[other],
            dst_ref=code_recv.at[group],
            send_sem=code_sem.at[0],
            recv_sem=code_sem.at[1],
            device_id=(other, me),
            device_id_type=MESH,
        )

    def side_copy(other):
        return pltpu.make_async_remote_copy(
            src_ref=side_send.at[other],
            dst_ref=side_recv.at[group],
            send_sem=side_sem.at[0],
            recv_sem=side_sem.at[1],
            device_id=(other, me),
            device_id_type=MESH,
        )

    all_blocks(send2, recv2, send2_sem, recv2_sem, 1).wait_recv()

    def pack_step(block, carry):
        here = pl.ds(pl.multiple_of(block * tall, tall), tall)
        row_grads = picked_grads[here, :] + jnp.dot(
            picked_hit[here, part_rows:2 * part_rows],
            recv2[1].reshape(part_rows, width),
            preferred_element_type=jnp.float32,
        )
        new_rows, new_state = adagrad(picked_table[here, :], picked_state[here, :], row_grads)
        scale = jnp.maximum(jnp.max(jnp.abs(new_rows), axis=-1, keepdims=True), 1e-30)
        values = jnp.round(new_rows * (TOP / scale))
        values = values.astype(jnp.int32).astype(jnp.int16).reshape(band, CAP, width)
        at = lax.broadcasted_iota(jnp.int32, (tall, 128), 1)
        aside = jnp.where(at == 0, new_state, scale * (1.0 / TOP)).T
        for turn in range(band):
            k = block * band + turn
            other = dest(k)
            code_send[other] = values[turn]
            side_send[other, :, 0:CAP] = aside[0:2, turn * CAP:(turn + 1) * CAP]

            @pl.when(k != wing)
            def _():
                code_copy(other).start()
                side_copy(other).start()

        return carry

    lax.fori_loop(0, groups // band, pack_step, 0)
    stores = [
        pltpu.make_async_copy(source, target, store_sem.at[i])
        for i, (source, target) in enumerate((
            (code_send.at[group], code_recv.at[group]),
            (side_send.at[group], side_recv.at[group]),
            (new_table_ref, new_table_hbm),
            (new_state_ref, new_state_hbm),
        ))
    ]
    stores[0].start()
    stores[1].start()

    def update_step(block, carry):
        base = pl.multiple_of(block * row_block, row_block)
        here = pl.ds(base, row_block)
        row_grads = grads[here, :] + jnp.dot(
            hit[here, part_rows:2 * part_rows],
            recv2[1].reshape(part_rows, width),
            preferred_element_type=jnp.float32,
        )
        new_rows, new_state = adagrad(table_ref[here, :], state_col[here, :], row_grads)
        new_table_ref[here, :] = new_rows
        new_col[here, :] = new_state
        return carry

    lax.fori_loop(0, rows // row_block, update_step, 0)
    stores[2].start()
    new_state_ref[...] = new_col[...].T[0:1]
    stores[3].start()

    others = pl.ds(0, groups - 1)
    next_group = (group + 1) % groups
    all_codes = pltpu.make_async_remote_copy(
        src_ref=code_send.at[others],
        dst_ref=code_recv.at[others],
        send_sem=code_sem.at[0],
        recv_sem=code_sem.at[1],
        device_id=(next_group, me),
        device_id_type=MESH,
    )
    all_sides = pltpu.make_async_remote_copy(
        src_ref=side_send.at[others],
        dst_ref=side_recv.at[others],
        send_sem=side_sem.at[0],
        recv_sem=side_sem.at[1],
        device_id=(next_group, me),
        device_id_type=MESH,
    )
    for part in range(PARTS):
        all_blocks(send1, recv1, send1_sem, recv1_sem, part).wait_send()
        all_blocks(send2, recv2, send2_sem, recv2_sem, part).wait_send()
    for store in stores:
        store.wait()
    all_sides.wait_send()
    all_codes.wait_send()
    all_sides.wait_recv()
    all_codes.wait_recv()


def finish_kernel(
    table_hbm, state_hbm, code_hbm, side_hbm,
    new_table_ref, new_state_ref, arrived_ref, arrived_state_ref,
    table_ref, state_ref, code_ref, side_ref, decoded, states, in_sems, out_sems,
):
    groups = code_ref.shape[0]
    pieces = 4
    band = groups // pieces
    rows = table_ref.shape[2] // pieces
    loads = [
        pltpu.make_async_copy(side_hbm, side_ref, in_sems.at[0]),
        pltpu.make_async_copy(state_hbm, state_ref.at[0], in_sems.at[1]),
    ]
    for block in range(pieces):
        here = pl.ds(block * band, band)
        loads.append(
            pltpu.make_async_copy(code_hbm.at[here], code_ref.at[here], in_sems.at[2 + block])
        )
    for block in range(pieces):
        here = pl.ds(block * rows, rows)
        loads.append(
            pltpu.make_async_copy(
                table_hbm.at[here], table_ref.at[0, 0, here], in_sems.at[2 + pieces + block]
            )
        )
    for load in loads:
        load.start()
    stores = []

    def store(source, target):
        copy = pltpu.make_async_copy(source, target, out_sems.at[len(stores)])
        copy.start()
        stores.append(copy)

    loads[0].wait()
    states[0] = side_ref[:, 0:1, 0:CAP]
    store(states, arrived_state_ref)
    scales = side_ref[:, 1, :].T
    loads[1].wait()
    store(state_ref, new_state_ref)
    for block in range(pieces):
        loads[2 + block].wait()
        for turn in range(band):
            h = block * band + turn
            decoded[0, h, 0] = code_ref[h].astype(jnp.float32) * scales[0:CAP, h:h + 1]
        here = pl.ds(block * band, band)
        store(decoded.at[0, here], arrived_ref.at[0, here])
    for block in range(pieces):
        here = pl.ds(block * rows, rows)
        loads[2 + pieces + block].wait()
        store(table_ref.at[0, 0, here], new_table_ref.at[0, 0, here])
    for copy in stores:
        copy.wait()


def on_device(table, row_state, bag_ids, bag_lengths, interaction_grad, move_rows):
    groups = lax.axis_size("group")
    shards = lax.axis_size("shard")
    line = 6 if shards % 6 == 0 else 2
    rows, width = table.shape[2:]
    slots, samples = bag_ids.shape[2:]
    deep = samples // shards // PARTS
    squares = jnp.transpose(interaction_grad[0], (0, 2, 1)).reshape(samples, shards)
    in_hbm = pl.BlockSpec(memory_space=pltpu.HBM)
    blocks = (PARTS, shards, deep, width)
    bf16, f32, i32, i16 = jnp.bfloat16, jnp.float32, jnp.int32, jnp.int16
    lanes = (shards * deep, width // 2)
    moved = groups * CAP
    pair = pltpu.SemaphoreType.DMA((2,))
    new_table, new_state, code, side = pl.pallas_call(
        functools.partial(bag_kernel, groups, shards, line),
        name="bags",
        out_shape=(
            jax.ShapeDtypeStruct((rows, width), f32),
            jax.ShapeDtypeStruct((1, rows), f32),
            jax.ShapeDtypeStruct((groups, CAP, width), i16),
            jax.ShapeDtypeStruct((groups, 2, 128), f32),
        ),
        in_specs=[in_hbm] * 6,
        out_specs=(in_hbm,) * 4,
        scratch_shapes=[
            pltpu.VMEM((rows, width), f32),
            pltpu.VMEM((1, rows), f32),
            pltpu.VMEM((slots, samples), i32),
            pltpu.VMEM((1, samples), i32),
            pltpu.VMEM((samples, shards), f32),
            pltpu.SMEM((1, groups), i32),
            pltpu.VMEM((PARTS, shards, deep, 8), i32),
            pltpu.VMEM((8, samples), i32),
            pltpu.VMEM((rows, 3 * width), bf16),
            pltpu.VMEM((rows, 128), bf16),
            pltpu.VMEM((rows, samples), bf16),
            pltpu.VMEM((moved, samples), bf16),
            pltpu.VMEM((PARTS * deep, 3 * shards, shards), bf16),
            pltpu.VMEM(blocks, bf16),
            pltpu.VMEM(blocks, bf16),
            pltpu.VMEM(blocks, bf16),
            pltpu.VMEM(blocks, bf16),
            pltpu.VMEM(lanes, f32),
            pltpu.VMEM(lanes, f32),
            pltpu.VMEM(lanes, f32),
            pltpu.VMEM(lanes, f32),
            pltpu.VMEM((rows, width), f32),
            pltpu.VMEM((moved, width), f32),
            pltpu.VMEM((moved, width), f32),
            pltpu.VMEM((moved, 128), f32),
            pltpu.VMEM((rows, 128), f32),
            pltpu.VMEM((rows, 128), f32),
            pltpu.VMEM((rows, width), f32),
            pltpu.VMEM((1, rows), f32),
            pltpu.VMEM((groups, CAP, width), i16),
            pltpu.VMEM((groups, 2, 128), f32),
            pltpu.SMEM((groups,), i32),
            pltpu.SemaphoreType.DMA((6,)),
            pltpu.SemaphoreType.DMA((4,)),
            pair, pair, pair, pair, pair, pair,
        ],
        compiler_params=pltpu.CompilerParams(
            collective_id=0, has_side_effects=True, vmem_limit_bytes=VMEM_BYTES
        ),
        cost_estimate=pl.CostEstimate(
            flops=12 * samples * rows * width, bytes_accessed=6 * rows * width * 4, transcendentals=0
        ),
    )(
        table[0, 0],
        row_state[0],
        bag_ids[0, 0],
        bag_lengths[0],
        squares,
        move_rows[0],
    )
    return pl.pallas_call(
        finish_kernel,
        name="finish",
        out_shape=(
            jax.ShapeDtypeStruct((1, 1, rows, width), f32),
            jax.ShapeDtypeStruct((1, 1, rows), f32),
            jax.ShapeDtypeStruct((1, groups, 1, CAP, width), f32),
            jax.ShapeDtypeStruct((1, groups, 1, CAP), f32),
        ),
        in_specs=[in_hbm] * 4,
        out_specs=(in_hbm,) * 4,
        scratch_shapes=[
            pltpu.VMEM((1, 1, rows, width), f32),
            pltpu.VMEM((1, 1, rows), f32),
            pltpu.VMEM((groups, CAP, width), i16),
            pltpu.VMEM((groups, 2, 128), f32),
            pltpu.VMEM((1, groups, 1, CAP, width), f32),
            pltpu.VMEM((1, groups, 1, CAP), f32),
            pltpu.SemaphoreType.DMA((10,)),
            pltpu.SemaphoreType.DMA((10,)),
        ],
        compiler_params=pltpu.CompilerParams(vmem_limit_bytes=VMEM_BYTES),
        cost_estimate=pl.CostEstimate(
            flops=rows * width, bytes_accessed=10 * rows * width, transcendentals=0
        ),
    )(new_table, new_state, code, side)


def solution(mesh):
    in_specs = (
        P("group", "shard", None, None),
        P("group", "shard", None),
        P("group", "shard", None, None),
        P("group", "shard", None),
        P("group", None, None, "shard"),
        P("group", "shard", None),
    )
    out_specs = (
        P("group", "shard", None, None),
        P("group", "shard", None),
        P("group", None, "shard", None, None),
        P("group", None, "shard", None),
    )
    return jax.shard_map(
        on_device, mesh=mesh, in_specs=in_specs, out_specs=out_specs, check_vma=False
    )
```

```python
import functools

import jax
import jax.numpy as jnp
from jax import lax
from jax.experimental import pallas as pl
from jax.experimental.pallas import tpu as pltpu
from jax.sharding import PartitionSpec as P

MESH = pl.DeviceIdType.MESH
CAP = 64
PARTS = 2
TOP = 32767.0
VMEM_BYTES = 60 * 1024 * 1024
SPOTS = (0, 1, 2, 3, 4, 5)

learn_rate = 0.05
epsilon = 1e-08


def split_three(values):
    high = values.astype(jnp.bfloat16)
    rest = values - high.astype(jnp.float32)
    middle = rest.astype(jnp.bfloat16)
    low = (rest - middle.astype(jnp.float32)).astype(jnp.bfloat16)
    return high, middle, low


def bag_kernel(
    groups, shards, line,
    table_hbm, state_hbm, ids_hbm, len_hbm, grad_hbm, counts_hbm,
    new_table_hbm, new_state_hbm, code_recv, side_recv,
    table_ref, state_ref, ids_ref, len_ref, grad_ref, counts_ref,
    ids_col, ids_row, parts, state_parts, hit, picked_hit, mix, send1, recv1, send2, recv2,
    in_left, in_right, out_left, out_right, grads, picked_grads, picked_table, picked_state,
    state_col, new_col, new_table_ref, new_state_ref, code_send, side_send, starts,
    load_sem, store_sem, send1_sem, recv1_sem, send2_sem, recv2_sem, code_sem, side_sem,
):
    rows, width = table_ref.shape
    slots, samples = ids_ref.shape
    deep = samples // shards // PARTS
    half = width // 2
    part_rows = shards * deep
    lines = shards // line
    group = lax.axis_index("group")
    me = lax.axis_index("shard")
    my_line = me // line
    my_spot = me % line
    wing = groups // 2
    my_wing = group // wing
    my_place = group % wing

    loads = [
        pltpu.make_async_copy(source, target, load_sem.at[i])
        for i, (source, target) in enumerate((
            (ids_hbm, ids_ref),
            (len_hbm, len_ref),
            (table_hbm, table_ref),
            (grad_hbm, grad_ref),
            (state_hbm, state_ref),
            (counts_hbm, counts_ref),
        ))
    ]
    def dest(k):
        return ((my_wing + 1 + k // wing) % 2) * wing + (my_place + k) % wing

    barrier = pltpu.get_barrier_semaphore()

    def greet_shard(k, carry):
        pl.semaphore_signal(
            barrier, inc=1, device_id=(group, (me + k) % shards), device_id_type=MESH
        )
        return carry

    def greet_group(k, carry):
        pl.semaphore_signal(
            barrier, inc=1, device_id=((group + k) % groups, me), device_id_type=MESH
        )
        return carry

    lax.fori_loop(1, shards, greet_shard, 0)
    lax.fori_loop(1, groups, greet_group, 0)
    for load in loads:
        load.start()

    def block_copy(source, target, send_sem, recv_sem, part, other):
        return pltpu.make_async_remote_copy(
            src_ref=source.at[part, other],
            dst_ref=target.at[part, me],
            send_sem=send_sem.at[part],
            recv_sem=recv_sem.at[part],
            device_id=(group, other),
            device_id_type=MESH,
        )

    def all_blocks(source, target, send_sem, recv_sem, part):
        return pltpu.make_async_remote_copy(
            src_ref=source.at[part, pl.ds(0, shards - 1)],
            dst_ref=target.at[part, pl.ds(0, shards - 1)],
            send_sem=send_sem.at[part],
            recv_sem=recv_sem.at[part],
            device_id=(group, (me + 1) % shards),
            device_id_type=MESH,
        )

    def send_line(source, target, send_sem, recv_sem, part, step, first_turn):
        first = ((my_line + step) % lines) * line
        for turn in range(first_turn, line):
            other = first + (my_spot + turn) % line
            block_copy(source, target, send_sem, recv_sem, part, other).start()

    def send_spot(source, target, send_sem, recv_sem, part, spot):
        def spot_step(step, carry):
            other = ((my_line + step) % lines) * line + spot
            copy = block_copy(source, target, send_sem, recv_sem, part, other)
            pl.when(other != me)(copy.start)
            return carry

        lax.fori_loop(0, lines, spot_step, 0)

    loads[0].wait()
    loads[1].wait()
    slot = lax.broadcasted_iota(jnp.int32, (slots, samples), 0)
    live = jnp.where(slot < len_ref[...], ids_ref[...], -1)
    live = jnp.concatenate([live, jnp.full((8 - slots, samples), -1, jnp.int32)], axis=0)
    columns = live.T.reshape(lines, line, PARTS, deep, 8)
    for part in range(PARTS):
        ids_col[part] = columns[:, :, part]

    loads[2].wait()
    high, middle, low = split_three(table_ref[...])
    parts[:, 0:width] = high
    parts[:, width:2 * width] = middle
    parts[:, 2 * width:3 * width] = low

    def pool(column):
        lane = lax.broadcasted_iota(jnp.int32, (column.shape[0], rows), 1)
        total = jnp.zeros((column.shape[0], rows), jnp.float32)
        for j in range(slots):
            total = total + jnp.where(column[:, j:j + 1] == lane, 1.0, 0.0)
        product = jnp.dot(
            total.astype(jnp.bfloat16), parts[...], preferred_element_type=jnp.float32
        )
        pooled = product[:, 0:width] + product[:, width:2 * width]
        return (pooled + product[:, 2 * width:3 * width]).astype(jnp.bfloat16)

    def pool_line(part, step):
        at = (my_line + step) % lines
        pooled = pool(ids_col[part, at].reshape(line * deep, 8))
        send1[part, pl.ds(at * line, line)] = pooled.reshape(line, deep, width)

    def pool_spot(part, spot):
        pooled = pool(ids_col[part, :, spot].reshape(lines * deep, 8))
        for at in range(lines):
            send1[part, at * line + spot] = pooled[at * deep:(at + 1) * deep]

    def first_step(step, carry):
        pool_line(0, step)
        send_line(send1, recv1, send1_sem, recv1_sem, 0, step, 0)
        return carry

    pool_line(0, 0)
    pl.semaphore_wait(barrier, shards + groups - 2)
    send_line(send1, recv1, send1_sem, recv1_sem, 0, 0, 1)
    lax.fori_loop(1, lines, first_step, 0)
    recv1[0, me] = send1[0, me]

    def second_step(spot, carry):
        pool_spot(1, spot)
        send_spot(send1, recv1, send1_sem, recv1_sem, 1, spot)
        return carry

    lax.fori_loop(0, line, second_step, 0)
    recv1[1, me] = send1[1, me]

    loads[3].wait()

    def mix_step(b, carry):
        square = grad_ref[pl.ds(b, shards, stride=PARTS * deep), :]
        square = square + square.T
        first, second, third = split_three(square)
        mix[b] = jnp.concatenate([first, second, third], axis=0)
        return carry

    lax.fori_loop(0, PARTS * deep, mix_step, 0)

    def mix_part(part):
        all_blocks(send1, recv1, send1_sem, recv1_sem, part).wait_recv()
        block = recv1[part].reshape(part_rows, width).astype(jnp.float32)
        in_left[...] = block[:, :half]
        in_right[...] = block[:, half:]

        def sample_step(i, carry):
            inner = jnp.concatenate(
                [in_left[pl.ds(i, shards, stride=deep), :], in_right[pl.ds(i, shards, stride=deep), :]],
                axis=1,
            ).astype(jnp.bfloat16)
            product = jnp.dot(mix[part * deep + i], inner, preferred_element_type=jnp.float32)
            outer = product[0:shards] + product[shards:2 * shards] + product[2 * shards:3 * shards]
            out_left[pl.ds(i, shards, stride=deep), :] = outer[:, :half]
            out_right[pl.ds(i, shards, stride=deep), :] = outer[:, half:]
            return carry

        lax.fori_loop(0, deep, sample_step, 0)
        both = jnp.concatenate([out_left[...], out_right[...]], axis=1)
        send2[part] = both.astype(jnp.bfloat16).reshape(shards, deep, width)

        for spot in SPOTS if line == 6 else range(line):
            send_spot(send2, recv2, send2_sem, recv2_sem, part, spot)
        recv2[part, me] = send2[part, me]

    mix_part(0)

    ordered = jnp.concatenate([ids_col[part].reshape(part_rows, 8) for part in range(PARTS)], axis=0)
    ids_row[...] = ordered.T
    loads[4].wait()
    loads[5].wait()
    state_col[...] = jnp.broadcast_to(state_ref[...], (128, rows)).T
    acc = jnp.int32(0)
    for h in range(groups):
        starts[h] = acc
        acc = acc + counts_ref[0, h]
    lane = lax.broadcasted_iota(jnp.int32, (rows, 128), 1)
    first, second, third = (piece.astype(jnp.float32) for piece in split_three(state_col[...]))
    state_parts[...] = jnp.where(
        lane == 0, first, jnp.where(lane == 1, second, jnp.where(lane == 2, third, 0.0))
    ).astype(jnp.bfloat16)

    band = 4 if groups % 4 == 0 else groups
    tall = band * CAP

    def goals(block):
        place = lax.broadcasted_iota(jnp.int32, (CAP, 128), 0)
        pieces = []
        for turn in range(band):
            other = dest(block * band + turn)
            pieces.append(jnp.where(place < counts_ref[0, other], place + starts[other], -2))
        return jnp.concatenate(pieces, axis=0)[:, 0:1]

    def count_hits(goal, size):
        total = jnp.zeros((size, samples), jnp.float32)
        for j in range(slots):
            total = total + jnp.where(ids_row[j:j + 1, :] == goal, 1.0, 0.0)
        return total.astype(jnp.bfloat16)

    def pick_step(block, carry):
        here = pl.ds(pl.multiple_of(block * tall, tall), tall)
        goal = goals(block)
        for piece in range(2):
            span = slice(piece * tall // 2, (piece + 1) * tall // 2)
            at = pl.ds(pl.multiple_of(block * tall + piece * tall // 2, tall // 2), tall // 2)
            picked_hit[at, :] = count_hits(goal[span], tall // 2)
        pick = jnp.where(
            goal == lax.broadcasted_iota(jnp.int32, (tall, rows), 1), 1.0, 0.0
        ).astype(jnp.bfloat16)
        product = jnp.dot(pick, parts[...], preferred_element_type=jnp.float32)
        both = product[:, 0:width] + product[:, width:2 * width]
        picked_table[here, :] = both + product[:, 2 * width:3 * width]
        product = jnp.dot(pick, state_parts[...], preferred_element_type=jnp.float32)
        total = (product[:, 0:1] + product[:, 1:2]) + product[:, 2:3]
        picked_state[here, :] = jnp.broadcast_to(total, (tall, 128))
        return carry

    lax.fori_loop(0, groups // band, pick_step, 0)

    mix_part(1)

    row_block = 128 if rows % 128 == 0 else rows

    def hit_step(block, carry):
        base = pl.multiple_of(block * row_block, row_block)
        row = lax.broadcasted_iota(jnp.int32, (row_block, samples), 0) + base
        hit[pl.ds(base, row_block), :] = count_hits(row, row_block)
        return carry

    lax.fori_loop(0, rows // row_block, hit_step, 0)
    side_send[...] = jnp.zeros(side_send.shape, jnp.float32)

    all_blocks(send2, recv2, send2_sem, recv2_sem, 0).wait_recv()
    returned = recv2[0].reshape(part_rows, width)
    picked_grads[...] = jnp.dot(
        picked_hit[:, 0:part_rows], returned, preferred_element_type=jnp.float32
    )
    grads[...] = jnp.dot(hit[:, 0:part_rows], returned, preferred_element_type=jnp.float32)

    def adagrad(old_rows, old_state, row_grads):
        square = jnp.sum(row_grads * row_grads, axis=-1, keepdims=True) * (1.0 / width)
        new_state = old_state + square
        step = learn_rate / (jnp.sqrt(new_state) + epsilon)
        return old_rows - row_grads * step[:, 0:1], new_state

    def code_copy(other):
        return pltpu.make_async_remote_copy(
            src_ref=code_send.at[other],
            dst_ref=code_recv.at[group],
            send_sem=code_sem.at[0],
            recv_sem=code_sem.at[1],
            device_id=(other, me),
            device_id_type=MESH,
        )

    def side_copy(other):
        return pltpu.make_async_remote_copy(
            src_ref=side_send.at[other],
            dst_ref=side_recv.at[group],
            send_sem=side_sem.at[0],
            recv_sem=side_sem.at[1],
            device_id=(other, me),
            device_id_type=MESH,
        )

    all_blocks(send2, recv2, send2_sem, recv2_sem, 1).wait_recv()

    def pack_step(block, carry):
        here = pl.ds(pl.multiple_of(block * tall, tall), tall)
        row_grads = picked_grads[here, :] + jnp.dot(
            picked_hit[here, part_rows:2 * part_rows],
            recv2[1].reshape(part_rows, width),
            preferred_element_type=jnp.float32,
        )
        new_rows, new_state = adagrad(picked_table[here, :], picked_state[here, :], row_grads)
        scale = jnp.maximum(jnp.max(jnp.abs(new_rows), axis=-1, keepdims=True), 1e-30)
        values = jnp.round(new_rows * (TOP / scale))
        values = values.astype(jnp.int32).astype(jnp.int16).reshape(band, CAP, width)
        at = lax.broadcasted_iota(jnp.int32, (tall, 128), 1)
        aside = jnp.where(at == 0, new_state, scale * (1.0 / TOP)).T
        for turn in range(band):
            k = block * band + turn
            other = dest(k)
            code_send[other] = values[turn]
            side_send[other, :, 0:CAP] = aside[0:2, turn * CAP:(turn + 1) * CAP]

            @pl.when(k != wing)
            def _():
                code_copy(other).start()
                side_copy(other).start()

        return carry

    lax.fori_loop(0, groups // band, pack_step, 0)
    stores = [
        pltpu.make_async_copy(source, target, store_sem.at[i])
        for i, (source, target) in enumerate((
            (code_send.at[group], code_recv.at[group]),
            (side_send.at[group], side_recv.at[group]),
            (new_table_ref, new_table_hbm),
            (new_state_ref, new_state_hbm),
        ))
    ]
    stores[0].start()
    stores[1].start()

    def update_step(block, carry):
        base = pl.multiple_of(block * row_block, row_block)
        here = pl.ds(base, row_block)
        row_grads = grads[here, :] + jnp.dot(
            hit[here, part_rows:2 * part_rows],
            recv2[1].reshape(part_rows, width),
            preferred_element_type=jnp.float32,
        )
        new_rows, new_state = adagrad(table_ref[here, :], state_col[here, :], row_grads)
        new_table_ref[here, :] = new_rows
        new_col[here, :] = new_state
        return carry

    lax.fori_loop(0, rows // row_block, update_step, 0)
    stores[2].start()
    new_state_ref[...] = new_col[...].T[0:1]
    stores[3].start()

    others = pl.ds(0, groups - 1)
    next_group = (group + 1) % groups
    all_codes = pltpu.make_async_remote_copy(
        src_ref=code_send.at[others],
        dst_ref=code_recv.at[others],
        send_sem=code_sem.at[0],
        recv_sem=code_sem.at[1],
        device_id=(next_group, me),
        device_id_type=MESH,
    )
    all_sides = pltpu.make_async_remote_copy(
        src_ref=side_send.at[others],
        dst_ref=side_recv.at[others],
        send_sem=side_sem.at[0],
        recv_sem=side_sem.at[1],
        device_id=(next_group, me),
        device_id_type=MESH,
    )
    for part in range(PARTS):
        all_blocks(send1, recv1, send1_sem, recv1_sem, part).wait_send()
        all_blocks(send2, recv2, send2_sem, recv2_sem, part).wait_send()
    for store in stores:
        store.wait()
    all_sides.wait_send()
    all_codes.wait_send()
    all_sides.wait_recv()
    all_codes.wait_recv()


def finish_kernel(
    table_hbm, state_hbm, code_hbm, side_hbm,
    new_table_ref, new_state_ref, arrived_ref, arrived_state_ref,
    table_ref, state_ref, code_ref, side_ref, decoded, states, in_sems, out_sems,
):
    groups = code_ref.shape[0]
    pieces = 4
    band = groups // pieces
    rows = table_ref.shape[2] // pieces
    loads = [
        pltpu.make_async_copy(side_hbm, side_ref, in_sems.at[0]),
        pltpu.make_async_copy(state_hbm, state_ref.at[0], in_sems.at[1]),
    ]
    for block in range(pieces):
        here = pl.ds(block * band, band)
        loads.append(
            pltpu.make_async_copy(code_hbm.at[here], code_ref.at[here], in_sems.at[2 + block])
        )
    for block in range(pieces):
        here = pl.ds(block * rows, rows)
        loads.append(
            pltpu.make_async_copy(
                table_hbm.at[here], table_ref.at[0, 0, here], in_sems.at[2 + pieces + block]
            )
        )
    for load in loads:
        load.start()
    stores = []

    def store(source, target):
        copy = pltpu.make_async_copy(source, target, out_sems.at[len(stores)])
        copy.start()
        stores.append(copy)

    loads[0].wait()
    states[0] = side_ref[:, 0:1, 0:CAP]
    store(states, arrived_state_ref)
    scales = side_ref[:, 1, :].T
    loads[1].wait()
    store(state_ref, new_state_ref)
    for block in range(pieces):
        loads[2 + block].wait()
        for turn in range(band):
            h = block * band + turn
            decoded[0, h, 0] = code_ref[h].astype(jnp.float32) * scales[0:CAP, h:h + 1]
        here = pl.ds(block * band, band)
        store(decoded.at[0, here], arrived_ref.at[0, here])
    for block in range(pieces):
        here = pl.ds(block * rows, rows)
        loads[2 + pieces + block].wait()
        store(table_ref.at[0, 0, here], new_table_ref.at[0, 0, here])
    for copy in stores:
        copy.wait()


def on_device(table, row_state, bag_ids, bag_lengths, interaction_grad, move_rows):
    groups = lax.axis_size("group")
    shards = lax.axis_size("shard")
    line = 6 if shards % 6 == 0 else 2
    rows, width = table.shape[2:]
    slots, samples = bag_ids.shape[2:]
    deep = samples // shards // PARTS
    squares = jnp.transpose(interaction_grad[0], (0, 2, 1)).reshape(samples, shards)
    in_hbm = pl.BlockSpec(memory_space=pltpu.HBM)
    blocks = (PARTS, shards, deep, width)
    bf16, f32, i32, i16 = jnp.bfloat16, jnp.float32, jnp.int32, jnp.int16
    lanes = (shards * deep, width // 2)
    moved = groups * CAP
    pair = pltpu.SemaphoreType.DMA((2,))
    new_table, new_state, code, side = pl.pallas_call(
        functools.partial(bag_kernel, groups, shards, line),
        name="bags",
        out_shape=(
            jax.ShapeDtypeStruct((rows, width), f32),
            jax.ShapeDtypeStruct((1, rows), f32),
            jax.ShapeDtypeStruct((groups, CAP, width), i16),
            jax.ShapeDtypeStruct((groups, 2, 128), f32),
        ),
        in_specs=[in_hbm] * 6,
        out_specs=(in_hbm,) * 4,
        scratch_shapes=[
            pltpu.VMEM((rows, width), f32),
            pltpu.VMEM((1, rows), f32),
            pltpu.VMEM((slots, samples), i32),
            pltpu.VMEM((1, samples), i32),
            pltpu.VMEM((samples, shards), f32),
            pltpu.SMEM((1, groups), i32),
            pltpu.VMEM((PARTS, shards // line, line, deep, 8), i32),
            pltpu.VMEM((8, samples), i32),
            pltpu.VMEM((rows, 3 * width), bf16),
            pltpu.VMEM((rows, 128), bf16),
            pltpu.VMEM((rows, samples), bf16),
            pltpu.VMEM((moved, samples), bf16),
            pltpu.VMEM((PARTS * deep, 3 * shards, shards), bf16),
            pltpu.VMEM(blocks, bf16),
            pltpu.VMEM(blocks, bf16),
            pltpu.VMEM(blocks, bf16),
            pltpu.VMEM(blocks, bf16),
            pltpu.VMEM(lanes, f32),
            pltpu.VMEM(lanes, f32),
            pltpu.VMEM(lanes, f32),
            pltpu.VMEM(lanes, f32),
            pltpu.VMEM((rows, width), f32),
            pltpu.VMEM((moved, width), f32),
            pltpu.VMEM((moved, width), f32),
            pltpu.VMEM((moved, 128), f32),
            pltpu.VMEM((rows, 128), f32),
            pltpu.VMEM((rows, 128), f32),
            pltpu.VMEM((rows, width), f32),
            pltpu.VMEM((1, rows), f32),
            pltpu.VMEM((groups, CAP, width), i16),
            pltpu.VMEM((groups, 2, 128), f32),
            pltpu.SMEM((groups,), i32),
            pltpu.SemaphoreType.DMA((6,)),
            pltpu.SemaphoreType.DMA((4,)),
            pair, pair, pair, pair, pair, pair,
        ],
        compiler_params=pltpu.CompilerParams(
            collective_id=0, has_side_effects=True, vmem_limit_bytes=VMEM_BYTES
        ),
        cost_estimate=pl.CostEstimate(
            flops=12 * samples * rows * width, bytes_accessed=6 * rows * width * 4, transcendentals=0
        ),
    )(
        table[0, 0],
        row_state[0],
        bag_ids[0, 0],
        bag_lengths[0],
        squares,
        move_rows[0],
    )
    return pl.pallas_call(
        finish_kernel,
        name="finish",
        out_shape=(
            jax.ShapeDtypeStruct((1, 1, rows, width), f32),
            jax.ShapeDtypeStruct((1, 1, rows), f32),
            jax.ShapeDtypeStruct((1, groups, 1, CAP, width), f32),
            jax.ShapeDtypeStruct((1, groups, 1, CAP), f32),
        ),
        in_specs=[in_hbm] * 4,
        out_specs=(in_hbm,) * 4,
        scratch_shapes=[
            pltpu.VMEM((1, 1, rows, width), f32),
            pltpu.VMEM((1, 1, rows), f32),
            pltpu.VMEM((groups, CAP, width), i16),
            pltpu.VMEM((groups, 2, 128), f32),
            pltpu.VMEM((1, groups, 1, CAP, width), f32),
            pltpu.VMEM((1, groups, 1, CAP), f32),
            pltpu.SemaphoreType.DMA((10,)),
            pltpu.SemaphoreType.DMA((10,)),
        ],
        compiler_params=pltpu.CompilerParams(vmem_limit_bytes=VMEM_BYTES),
        cost_estimate=pl.CostEstimate(
            flops=rows * width, bytes_accessed=10 * rows * width, transcendentals=0
        ),
    )(new_table, new_state, code, side)


def solution(mesh):
    in_specs = (
        P("group", "shard", None, None),
        P("group", "shard", None),
        P("group", "shard", None, None),
        P("group", "shard", None),
        P("group", None, None, "shard"),
        P("group", "shard", None),
    )
    out_specs = (
        P("group", "shard", None, None),
        P("group", "shard", None),
        P("group", None, "shard", None, None),
        P("group", None, "shard", None),
    )
    return jax.shard_map(
        on_device, mesh=mesh, in_specs=in_specs, out_specs=out_specs, check_vma=False
    )
```

```python
import functools

import jax
import jax.numpy as jnp
from jax import lax
from jax.experimental import pallas as pl
from jax.experimental.pallas import tpu as pltpu
from jax.sharding import PartitionSpec as P

MESH = pl.DeviceIdType.MESH
CAP = 64
PARTS = 2
TOP = 32767.0
VMEM_BYTES = 60 * 1024 * 1024
SPOTS = (0, 1, 2, 3, 5, 4)

learn_rate = 0.05
epsilon = 1e-08


def split_three(values):
    high = values.astype(jnp.bfloat16)
    rest = values - high.astype(jnp.float32)
    middle = rest.astype(jnp.bfloat16)
    low = (rest - middle.astype(jnp.float32)).astype(jnp.bfloat16)
    return high, middle, low


def bag_kernel(
    groups, shards, line,
    table_hbm, state_hbm, ids_hbm, len_hbm, grad_hbm, counts_hbm,
    new_table_hbm, new_state_hbm, code_recv, side_recv,
    table_ref, state_ref, ids_ref, len_ref, grad_ref, counts_ref,
    ids_col, ids_row, parts, state_parts, hit, picked_hit, mix, send1, recv1, send2, recv2,
    in_left, in_right, out_left, out_right, grads, picked_grads, picked_table, picked_state,
    state_col, new_col, new_table_ref, new_state_ref, code_send, side_send, starts,
    load_sem, store_sem, send1_sem, recv1_sem, send2_sem, recv2_sem, code_sem, side_sem,
):
    rows, width = table_ref.shape
    slots, samples = ids_ref.shape
    deep = samples // shards // PARTS
    half = width // 2
    part_rows = shards * deep
    lines = shards // line
    group = lax.axis_index("group")
    me = lax.axis_index("shard")
    my_line = me // line
    my_spot = me % line
    wing = groups // 2
    my_wing = group // wing
    my_place = group % wing

    loads = [
        pltpu.make_async_copy(source, target, load_sem.at[i])
        for i, (source, target) in enumerate((
            (ids_hbm, ids_ref),
            (len_hbm, len_ref),
            (table_hbm, table_ref),
            (grad_hbm, grad_ref),
            (state_hbm, state_ref),
            (counts_hbm, counts_ref),
        ))
    ]
    def dest(k):
        return ((my_wing + 1 + k // wing) % 2) * wing + (my_place + k) % wing

    barrier = pltpu.get_barrier_semaphore()

    def greet_shard(k, carry):
        pl.semaphore_signal(
            barrier, inc=1, device_id=(group, (me + k) % shards), device_id_type=MESH
        )
        return carry

    def greet_group(k, carry):
        pl.semaphore_signal(
            barrier, inc=1, device_id=((group + k) % groups, me), device_id_type=MESH
        )
        return carry

    lax.fori_loop(1, shards, greet_shard, 0)
    lax.fori_loop(1, groups, greet_group, 0)
    for load in loads:
        load.start()

    def block_copy(source, target, send_sem, recv_sem, part, other):
        return pltpu.make_async_remote_copy(
            src_ref=source.at[part, other],
            dst_ref=target.at[part, me],
            send_sem=send_sem.at[part],
            recv_sem=recv_sem.at[part],
            device_id=(group, other),
            device_id_type=MESH,
        )

    def all_blocks(source, target, send_sem, recv_sem, part):
        return pltpu.make_async_remote_copy(
            src_ref=source.at[part, pl.ds(0, shards - 1)],
            dst_ref=target.at[part, pl.ds(0, shards - 1)],
            send_sem=send_sem.at[part],
            recv_sem=recv_sem.at[part],
            device_id=(group, (me + 1) % shards),
            device_id_type=MESH,
        )

    def send_line(source, target, send_sem, recv_sem, part, step, first_turn):
        first = ((my_line + step) % lines) * line
        for turn in range(first_turn, line):
            other = first + (my_spot + turn) % line
            block_copy(source, target, send_sem, recv_sem, part, other).start()

    def send_spot(source, target, send_sem, recv_sem, part, spot):
        def spot_step(step, carry):
            other = ((my_line + step) % lines) * line + spot
            copy = block_copy(source, target, send_sem, recv_sem, part, other)
            pl.when(other != me)(copy.start)
            return carry

        lax.fori_loop(0, lines, spot_step, 0)

    loads[0].wait()
    loads[1].wait()
    slot = lax.broadcasted_iota(jnp.int32, (slots, samples), 0)
    live = jnp.where(slot < len_ref[...], ids_ref[...], -1)
    live = jnp.concatenate([live, jnp.full((8 - slots, samples), -1, jnp.int32)], axis=0)
    columns = live.T.reshape(lines, line, PARTS, deep, 8)
    for part in range(PARTS):
        ids_col[part] = columns[:, :, part]

    loads[2].wait()
    high, middle, low = split_three(table_ref[...])
    parts[:, 0:width] = high
    parts[:, width:2 * width] = middle
    parts[:, 2 * width:3 * width] = low

    def pool(column):
        lane = lax.broadcasted_iota(jnp.int32, (column.shape[0], rows), 1)
        total = jnp.zeros((column.shape[0], rows), jnp.float32)
        for j in range(slots):
            total = total + jnp.where(column[:, j:j + 1] == lane, 1.0, 0.0)
        product = jnp.dot(
            total.astype(jnp.bfloat16), parts[...], preferred_element_type=jnp.float32
        )
        pooled = product[:, 0:width] + product[:, width:2 * width]
        return (pooled + product[:, 2 * width:3 * width]).astype(jnp.bfloat16)

    def pool_line(part, step):
        at = (my_line + step) % lines
        pooled = pool(ids_col[part, at].reshape(line * deep, 8))
        send1[part, pl.ds(at * line, line)] = pooled.reshape(line, deep, width)

    def pool_spot(part, spot):
        pooled = pool(ids_col[part, :, spot].reshape(lines * deep, 8))
        for at in range(lines):
            send1[part, at * line + spot] = pooled[at * deep:(at + 1) * deep]

    def first_step(step, carry):
        pool_line(0, step)
        send_line(send1, recv1, send1_sem, recv1_sem, 0, step, 0)
        return carry

    pool_line(0, 0)
    pl.semaphore_wait(barrier, shards + groups - 2)
    send_line(send1, recv1, send1_sem, recv1_sem, 0, 0, 1)
    lax.fori_loop(1, lines, first_step, 0)
    recv1[0, me] = send1[0, me]

    def second_step(spot, carry):
        pool_spot(1, spot)
        send_spot(send1, recv1, send1_sem, recv1_sem, 1, spot)
        return carry

    lax.fori_loop(0, line, second_step, 0)
    recv1[1, me] = send1[1, me]

    loads[3].wait()

    def mix_step(b, carry):
        square = grad_ref[pl.ds(b, shards, stride=PARTS * deep), :]
        square = square + square.T
        first, second, third = split_three(square)
        mix[b] = jnp.concatenate([first, second, third], axis=0)
        return carry

    lax.fori_loop(0, PARTS * deep, mix_step, 0)

    def mix_part(part):
        all_blocks(send1, recv1, send1_sem, recv1_sem, part).wait_recv()
        block = recv1[part].reshape(part_rows, width).astype(jnp.float32)
        in_left[...] = block[:, :half]
        in_right[...] = block[:, half:]

        def sample_step(i, carry):
            inner = jnp.concatenate(
                [in_left[pl.ds(i, shards, stride=deep), :], in_right[pl.ds(i, shards, stride=deep), :]],
                axis=1,
            ).astype(jnp.bfloat16)
            product = jnp.dot(mix[part * deep + i], inner, preferred_element_type=jnp.float32)
            outer = product[0:shards] + product[shards:2 * shards] + product[2 * shards:3 * shards]
            out_left[pl.ds(i, shards, stride=deep), :] = outer[:, :half]
            out_right[pl.ds(i, shards, stride=deep), :] = outer[:, half:]
            return carry

        lax.fori_loop(0, deep, sample_step, 0)
        both = jnp.concatenate([out_left[...], out_right[...]], axis=1)
        send2[part] = both.astype(jnp.bfloat16).reshape(shards, deep, width)

        for spot in SPOTS if line == 6 else range(line):
            send_spot(send2, recv2, send2_sem, recv2_sem, part, spot)
        recv2[part, me] = send2[part, me]

    mix_part(0)

    ordered = jnp.concatenate([ids_col[part].reshape(part_rows, 8) for part in range(PARTS)], axis=0)
    ids_row[...] = ordered.T
    loads[4].wait()
    loads[5].wait()
    state_col[...] = jnp.broadcast_to(state_ref[...], (128, rows)).T
    acc = jnp.int32(0)
    for h in range(groups):
        starts[h] = acc
        acc = acc + counts_ref[0, h]
    lane = lax.broadcasted_iota(jnp.int32, (rows, 128), 1)
    first, second, third = (piece.astype(jnp.float32) for piece in split_three(state_col[...]))
    state_parts[...] = jnp.where(
        lane == 0, first, jnp.where(lane == 1, second, jnp.where(lane == 2, third, 0.0))
    ).astype(jnp.bfloat16)

    band = 4 if groups % 4 == 0 else groups
    tall = band * CAP

    def goals(block):
        place = lax.broadcasted_iota(jnp.int32, (CAP, 128), 0)
        pieces = []
        for turn in range(band):
            other = dest(block * band + turn)
            pieces.append(jnp.where(place < counts_ref[0, other], place + starts[other], -2))
        return jnp.concatenate(pieces, axis=0)[:, 0:1]

    def count_hits(goal, size):
        total = jnp.zeros((size, samples), jnp.float32)
        for j in range(slots):
            total = total + jnp.where(ids_row[j:j + 1, :] == goal, 1.0, 0.0)
        return total.astype(jnp.bfloat16)

    def pick_step(block, carry):
        here = pl.ds(pl.multiple_of(block * tall, tall), tall)
        goal = goals(block)
        for piece in range(2):
            span = slice(piece * tall // 2, (piece + 1) * tall // 2)
            at = pl.ds(pl.multiple_of(block * tall + piece * tall // 2, tall // 2), tall // 2)
            picked_hit[at, :] = count_hits(goal[span], tall // 2)
        pick = jnp.where(
            goal == lax.broadcasted_iota(jnp.int32, (tall, rows), 1), 1.0, 0.0
        ).astype(jnp.bfloat16)
        product = jnp.dot(pick, parts[...], preferred_element_type=jnp.float32)
        both = product[:, 0:width] + product[:, width:2 * width]
        picked_table[here, :] = both + product[:, 2 * width:3 * width]
        product = jnp.dot(pick, state_parts[...], preferred_element_type=jnp.float32)
        total = (product[:, 0:1] + product[:, 1:2]) + product[:, 2:3]
        picked_state[here, :] = jnp.broadcast_to(total, (tall, 128))
        return carry

    lax.fori_loop(0, groups // band, pick_step, 0)

    mix_part(1)

    row_block = 128 if rows % 128 == 0 else rows

    def hit_step(block, carry):
        base = pl.multiple_of(block * row_block, row_block)
        row = lax.broadcasted_iota(jnp.int32, (row_block, samples), 0) + base
        hit[pl.ds(base, row_block), :] = count_hits(row, row_block)
        return carry

    lax.fori_loop(0, rows // row_block, hit_step, 0)
    side_send[...] = jnp.zeros(side_send.shape, jnp.float32)

    all_blocks(send2, recv2, send2_sem, recv2_sem, 0).wait_recv()
    returned = recv2[0].reshape(part_rows, width)
    picked_grads[...] = jnp.dot(
        picked_hit[:, 0:part_rows], returned, preferred_element_type=jnp.float32
    )
    grads[...] = jnp.dot(hit[:, 0:part_rows], returned, preferred_element_type=jnp.float32)

    def adagrad(old_rows, old_state, row_grads):
        square = jnp.sum(row_grads * row_grads, axis=-1, keepdims=True) * (1.0 / width)
        new_state = old_state + square
        step = learn_rate / (jnp.sqrt(new_state) + epsilon)
        return old_rows - row_grads * step[:, 0:1], new_state

    def code_copy(other):
        return pltpu.make_async_remote_copy(
            src_ref=code_send.at[other],
            dst_ref=code_recv.at[group],
            send_sem=code_sem.at[0],
            recv_sem=code_sem.at[1],
            device_id=(other, me),
            device_id_type=MESH,
        )

    def side_copy(other):
        return pltpu.make_async_remote_copy(
            src_ref=side_send.at[other],
            dst_ref=side_recv.at[group],
            send_sem=side_sem.at[0],
            recv_sem=side_sem.at[1],
            device_id=(other, me),
            device_id_type=MESH,
        )

    all_blocks(send2, recv2, send2_sem, recv2_sem, 1).wait_recv()

    def pack_step(block, carry):
        here = pl.ds(pl.multiple_of(block * tall, tall), tall)
        row_grads = picked_grads[here, :] + jnp.dot(
            picked_hit[here, part_rows:2 * part_rows],
            recv2[1].reshape(part_rows, width),
            preferred_element_type=jnp.float32,
        )
        new_rows, new_state = adagrad(picked_table[here, :], picked_state[here, :], row_grads)
        scale = jnp.maximum(jnp.max(jnp.abs(new_rows), axis=-1, keepdims=True), 1e-30)
        values = jnp.round(new_rows * (TOP / scale))
        values = values.astype(jnp.int32).astype(jnp.int16).reshape(band, CAP, width)
        at = lax.broadcasted_iota(jnp.int32, (tall, 128), 1)
        aside = jnp.where(at == 0, new_state, scale * (1.0 / TOP)).T
        for turn in range(band):
            k = block * band + turn
            other = dest(k)
            code_send[other] = values[turn]
            side_send[other, :, 0:CAP] = aside[0:2, turn * CAP:(turn + 1) * CAP]

            @pl.when(k != wing)
            def _():
                code_copy(other).start()
                side_copy(other).start()

        return carry

    lax.fori_loop(0, groups // band, pack_step, 0)
    stores = [
        pltpu.make_async_copy(source, target, store_sem.at[i])
        for i, (source, target) in enumerate((
            (code_send.at[group], code_recv.at[group]),
            (side_send.at[group], side_recv.at[group]),
            (new_table_ref, new_table_hbm),
            (new_state_ref, new_state_hbm),
        ))
    ]
    stores[0].start()
    stores[1].start()

    def update_step(block, carry):
        base = pl.multiple_of(block * row_block, row_block)
        here = pl.ds(base, row_block)
        row_grads = grads[here, :] + jnp.dot(
            hit[here, part_rows:2 * part_rows],
            recv2[1].reshape(part_rows, width),
            preferred_element_type=jnp.float32,
        )
        new_rows, new_state = adagrad(table_ref[here, :], state_col[here, :], row_grads)
        new_table_ref[here, :] = new_rows
        new_col[here, :] = new_state
        return carry

    lax.fori_loop(0, rows // row_block, update_step, 0)
    stores[2].start()
    new_state_ref[...] = new_col[...].T[0:1]
    stores[3].start()

    others = pl.ds(0, groups - 1)
    next_group = (group + 1) % groups
    all_codes = pltpu.make_async_remote_copy(
        src_ref=code_send.at[others],
        dst_ref=code_recv.at[others],
        send_sem=code_sem.at[0],
        recv_sem=code_sem.at[1],
        device_id=(next_group, me),
        device_id_type=MESH,
    )
    all_sides = pltpu.make_async_remote_copy(
        src_ref=side_send.at[others],
        dst_ref=side_recv.at[others],
        send_sem=side_sem.at[0],
        recv_sem=side_sem.at[1],
        device_id=(next_group, me),
        device_id_type=MESH,
    )
    for part in range(PARTS):
        all_blocks(send1, recv1, send1_sem, recv1_sem, part).wait_send()
        all_blocks(send2, recv2, send2_sem, recv2_sem, part).wait_send()
    for store in stores:
        store.wait()
    all_sides.wait_send()
    all_codes.wait_send()
    all_sides.wait_recv()
    all_codes.wait_recv()


def finish_kernel(
    table_hbm, state_hbm, code_hbm, side_hbm,
    new_table_ref, new_state_ref, arrived_ref, arrived_state_ref,
    table_ref, state_ref, code_ref, side_ref, decoded, states, in_sems, out_sems,
):
    groups = code_ref.shape[0]
    pieces = 4
    band = groups // pieces
    rows = table_ref.shape[2] // pieces
    loads = [
        pltpu.make_async_copy(side_hbm, side_ref, in_sems.at[0]),
        pltpu.make_async_copy(state_hbm, state_ref.at[0], in_sems.at[1]),
    ]
    for block in range(pieces):
        here = pl.ds(block * band, band)
        loads.append(
            pltpu.make_async_copy(code_hbm.at[here], code_ref.at[here], in_sems.at[2 + block])
        )
    for block in range(pieces):
        here = pl.ds(block * rows, rows)
        loads.append(
            pltpu.make_async_copy(
                table_hbm.at[here], table_ref.at[0, 0, here], in_sems.at[2 + pieces + block]
            )
        )
    for load in loads:
        load.start()
    stores = []

    def store(source, target):
        copy = pltpu.make_async_copy(source, target, out_sems.at[len(stores)])
        copy.start()
        stores.append(copy)

    loads[0].wait()
    states[0] = side_ref[:, 0:1, 0:CAP]
    store(states, arrived_state_ref)
    scales = side_ref[:, 1, :].T
    loads[1].wait()
    store(state_ref, new_state_ref)
    for block in range(pieces):
        loads[2 + block].wait()
        for turn in range(band):
            h = block * band + turn
            decoded[0, h, 0] = code_ref[h].astype(jnp.float32) * scales[0:CAP, h:h + 1]
        here = pl.ds(block * band, band)
        store(decoded.at[0, here], arrived_ref.at[0, here])
    for block in range(pieces):
        here = pl.ds(block * rows, rows)
        loads[2 + pieces + block].wait()
        store(table_ref.at[0, 0, here], new_table_ref.at[0, 0, here])
    for copy in stores:
        copy.wait()


def on_device(table, row_state, bag_ids, bag_lengths, interaction_grad, move_rows):
    groups = lax.axis_size("group")
    shards = lax.axis_size("shard")
    line = 6 if shards % 6 == 0 else 2
    rows, width = table.shape[2:]
    slots, samples = bag_ids.shape[2:]
    deep = samples // shards // PARTS
    squares = jnp.transpose(interaction_grad[0], (0, 2, 1)).reshape(samples, shards)
    in_hbm = pl.BlockSpec(memory_space=pltpu.HBM)
    blocks = (PARTS, shards, deep, width)
    bf16, f32, i32, i16 = jnp.bfloat16, jnp.float32, jnp.int32, jnp.int16
    lanes = (shards * deep, width // 2)
    moved = groups * CAP
    pair = pltpu.SemaphoreType.DMA((2,))
    new_table, new_state, code, side = pl.pallas_call(
        functools.partial(bag_kernel, groups, shards, line),
        name="bags",
        out_shape=(
            jax.ShapeDtypeStruct((rows, width), f32),
            jax.ShapeDtypeStruct((1, rows), f32),
            jax.ShapeDtypeStruct((groups, CAP, width), i16),
            jax.ShapeDtypeStruct((groups, 2, 128), f32),
        ),
        in_specs=[in_hbm] * 6,
        out_specs=(in_hbm,) * 4,
        scratch_shapes=[
            pltpu.VMEM((rows, width), f32),
            pltpu.VMEM((1, rows), f32),
            pltpu.VMEM((slots, samples), i32),
            pltpu.VMEM((1, samples), i32),
            pltpu.VMEM((samples, shards), f32),
            pltpu.SMEM((1, groups), i32),
            pltpu.VMEM((PARTS, shards // line, line, deep, 8), i32),
            pltpu.VMEM((8, samples), i32),
            pltpu.VMEM((rows, 3 * width), bf16),
            pltpu.VMEM((rows, 128), bf16),
            pltpu.VMEM((rows, samples), bf16),
            pltpu.VMEM((moved, samples), bf16),
            pltpu.VMEM((PARTS * deep, 3 * shards, shards), bf16),
            pltpu.VMEM(blocks, bf16),
            pltpu.VMEM(blocks, bf16),
            pltpu.VMEM(blocks, bf16),
            pltpu.VMEM(blocks, bf16),
            pltpu.VMEM(lanes, f32),
            pltpu.VMEM(lanes, f32),
            pltpu.VMEM(lanes, f32),
            pltpu.VMEM(lanes, f32),
            pltpu.VMEM((rows, width), f32),
            pltpu.VMEM((moved, width), f32),
            pltpu.VMEM((moved, width), f32),
            pltpu.VMEM((moved, 128), f32),
            pltpu.VMEM((rows, 128), f32),
            pltpu.VMEM((rows, 128), f32),
            pltpu.VMEM((rows, width), f32),
            pltpu.VMEM((1, rows), f32),
            pltpu.VMEM((groups, CAP, width), i16),
            pltpu.VMEM((groups, 2, 128), f32),
            pltpu.SMEM((groups,), i32),
            pltpu.SemaphoreType.DMA((6,)),
            pltpu.SemaphoreType.DMA((4,)),
            pair, pair, pair, pair, pair, pair,
        ],
        compiler_params=pltpu.CompilerParams(
            collective_id=0, has_side_effects=True, vmem_limit_bytes=VMEM_BYTES
        ),
        cost_estimate=pl.CostEstimate(
            flops=12 * samples * rows * width, bytes_accessed=6 * rows * width * 4, transcendentals=0
        ),
    )(
        table[0, 0],
        row_state[0],
        bag_ids[0, 0],
        bag_lengths[0],
        squares,
        move_rows[0],
    )
    return pl.pallas_call(
        finish_kernel,
        name="finish",
        out_shape=(
            jax.ShapeDtypeStruct((1, 1, rows, width), f32),
            jax.ShapeDtypeStruct((1, 1, rows), f32),
            jax.ShapeDtypeStruct((1, groups, 1, CAP, width), f32),
            jax.ShapeDtypeStruct((1, groups, 1, CAP), f32),
        ),
        in_specs=[in_hbm] * 4,
        out_specs=(in_hbm,) * 4,
        scratch_shapes=[
            pltpu.VMEM((1, 1, rows, width), f32),
            pltpu.VMEM((1, 1, rows), f32),
            pltpu.VMEM((groups, CAP, width), i16),
            pltpu.VMEM((groups, 2, 128), f32),
            pltpu.VMEM((1, groups, 1, CAP, width), f32),
            pltpu.VMEM((1, groups, 1, CAP), f32),
            pltpu.SemaphoreType.DMA((10,)),
            pltpu.SemaphoreType.DMA((10,)),
        ],
        compiler_params=pltpu.CompilerParams(vmem_limit_bytes=VMEM_BYTES),
        cost_estimate=pl.CostEstimate(
            flops=rows * width, bytes_accessed=10 * rows * width, transcendentals=0
        ),
    )(new_table, new_state, code, side)


def solution(mesh):
    in_specs = (
        P("group", "shard", None, None),
        P("group", "shard", None),
        P("group", "shard", None, None),
        P("group", "shard", None),
        P("group", None, None, "shard"),
        P("group", "shard", None),
    )
    out_specs = (
        P("group", "shard", None, None),
        P("group", "shard", None),
        P("group", None, "shard", None, None),
        P("group", None, "shard", None),
    )
    return jax.shard_map(
        on_device, mesh=mesh, in_specs=in_specs, out_specs=out_specs, check_vma=False
    )
```

```python
import functools

import jax
import jax.numpy as jnp
from jax import lax
from jax.experimental import pallas as pl
from jax.experimental.pallas import tpu as pltpu
from jax.sharding import PartitionSpec as P

MESH = pl.DeviceIdType.MESH
CAP = 64
PARTS = 2
TOP = 32767.0
VMEM_BYTES = 60 * 1024 * 1024
SPOTS = (0, 1, 2, 3, 5, 4)

learn_rate = 0.05
epsilon = 1e-08


def split_three(values):
    high = values.astype(jnp.bfloat16)
    rest = values - high.astype(jnp.float32)
    middle = rest.astype(jnp.bfloat16)
    low = (rest - middle.astype(jnp.float32)).astype(jnp.bfloat16)
    return high, middle, low


def bag_kernel(
    groups, shards, line,
    table_hbm, state_hbm, ids_hbm, len_hbm, grad_hbm, counts_hbm,
    new_table_hbm, new_state_hbm, code_recv, side_recv,
    table_ref, state_ref, ids_ref, len_ref, grad_ref, counts_ref,
    ids_col, ids_row, parts, state_parts, hit, picked_hit, mix, send1, recv1, send2, recv2,
    in_left, in_right, out_left, out_right, grads, picked_grads, picked_table, picked_state,
    state_col, new_col, new_table_ref, new_state_ref, code_send, side_send, starts,
    load_sem, store_sem, send1_sem, recv1_sem, send2_sem, recv2_sem, code_sem, side_sem,
):
    rows, width = table_ref.shape
    slots, samples = ids_ref.shape
    deep = samples // shards // PARTS
    half = width // 2
    part_rows = shards * deep
    lines = shards // line
    group = lax.axis_index("group")
    me = lax.axis_index("shard")
    my_line = me // line
    my_spot = me % line
    wing = groups // 2
    my_place = group % wing

    loads = [
        pltpu.make_async_copy(source, target, load_sem.at[i])
        for i, (source, target) in enumerate((
            (ids_hbm, ids_ref),
            (len_hbm, len_ref),
            (table_hbm, table_ref),
            (grad_hbm, grad_ref),
            (state_hbm, state_ref),
            (counts_hbm, counts_ref),
        ))
    ]
    def dest(k):
        return (k // wing) * wing + (my_place + k) % wing

    barrier = pltpu.get_barrier_semaphore()

    def greet_shard(k, carry):
        pl.semaphore_signal(
            barrier, inc=1, device_id=(group, (me + k) % shards), device_id_type=MESH
        )
        return carry

    def greet_group(k, carry):
        pl.semaphore_signal(
            barrier, inc=1, device_id=((group + k) % groups, me), device_id_type=MESH
        )
        return carry

    lax.fori_loop(1, shards, greet_shard, 0)
    lax.fori_loop(1, groups, greet_group, 0)
    for load in loads:
        load.start()

    def block_copy(source, target, send_sem, recv_sem, part, other):
        return pltpu.make_async_remote_copy(
            src_ref=source.at[part, other],
            dst_ref=target.at[part, me],
            send_sem=send_sem.at[part],
            recv_sem=recv_sem.at[part],
            device_id=(group, other),
            device_id_type=MESH,
        )

    def all_blocks(source, target, send_sem, recv_sem, part):
        return pltpu.make_async_remote_copy(
            src_ref=source.at[part, pl.ds(0, shards - 1)],
            dst_ref=target.at[part, pl.ds(0, shards - 1)],
            send_sem=send_sem.at[part],
            recv_sem=recv_sem.at[part],
            device_id=(group, (me + 1) % shards),
            device_id_type=MESH,
        )

    def send_line(source, target, send_sem, recv_sem, part, step, first_turn):
        first = ((my_line + step) % lines) * line
        for turn in range(first_turn, line):
            other = first + (my_spot + turn) % line
            block_copy(source, target, send_sem, recv_sem, part, other).start()

    def send_spot(source, target, send_sem, recv_sem, part, spot):
        def spot_step(step, carry):
            other = ((my_line + step) % lines) * line + spot
            copy = block_copy(source, target, send_sem, recv_sem, part, other)
            pl.when(other != me)(copy.start)
            return carry

        lax.fori_loop(0, lines, spot_step, 0)

    loads[0].wait()
    loads[1].wait()
    slot = lax.broadcasted_iota(jnp.int32, (slots, samples), 0)
    live = jnp.where(slot < len_ref[...], ids_ref[...], -1)
    live = jnp.concatenate([live, jnp.full((8 - slots, samples), -1, jnp.int32)], axis=0)
    columns = live.T.reshape(lines, line, PARTS, deep, 8)
    for part in range(PARTS):
        ids_col[part] = columns[:, :, part]

    loads[2].wait()
    high, middle, low = split_three(table_ref[...])
    parts[:, 0:width] = high
    parts[:, width:2 * width] = middle
    parts[:, 2 * width:3 * width] = low

    def pool(column):
        lane = lax.broadcasted_iota(jnp.int32, (column.shape[0], rows), 1)
        total = jnp.zeros((column.shape[0], rows), jnp.float32)
        for j in range(slots):
            total = total + jnp.where(column[:, j:j + 1] == lane, 1.0, 0.0)
        product = jnp.dot(
            total.astype(jnp.bfloat16), parts[...], preferred_element_type=jnp.float32
        )
        pooled = product[:, 0:width] + product[:, width:2 * width]
        return (pooled + product[:, 2 * width:3 * width]).astype(jnp.bfloat16)

    def pool_line(part, step):
        at = (my_line + step) % lines
        pooled = pool(ids_col[part, at].reshape(line * deep, 8))
        send1[part, pl.ds(at * line, line)] = pooled.reshape(line, deep, width)

    def pool_spot(part, spot):
        pooled = pool(ids_col[part, :, spot].reshape(lines * deep, 8))
        for at in range(lines):
            send1[part, at * line + spot] = pooled[at * deep:(at + 1) * deep]

    def first_step(step, carry):
        pool_line(0, step)
        send_line(send1, recv1, send1_sem, recv1_sem, 0, step, 0)
        return carry

    pool_line(0, 0)
    pl.semaphore_wait(barrier, shards + groups - 2)
    send_line(send1, recv1, send1_sem, recv1_sem, 0, 0, 1)
    lax.fori_loop(1, lines, first_step, 0)
    recv1[0, me] = send1[0, me]

    def second_step(spot, carry):
        pool_spot(1, spot)
        send_spot(send1, recv1, send1_sem, recv1_sem, 1, spot)
        return carry

    lax.fori_loop(0, line, second_step, 0)
    recv1[1, me] = send1[1, me]

    loads[3].wait()

    def mix_step(b, carry):
        square = grad_ref[pl.ds(b, shards, stride=PARTS * deep), :]
        square = square + square.T
        first, second, third = split_three(square)
        mix[b] = jnp.concatenate([first, second, third], axis=0)
        return carry

    lax.fori_loop(0, PARTS * deep, mix_step, 0)

    def mix_part(part):
        all_blocks(send1, recv1, send1_sem, recv1_sem, part).wait_recv()
        block = recv1[part].reshape(part_rows, width).astype(jnp.float32)
        in_left[...] = block[:, :half]
        in_right[...] = block[:, half:]

        def sample_step(i, carry):
            inner = jnp.concatenate(
                [in_left[pl.ds(i, shards, stride=deep), :], in_right[pl.ds(i, shards, stride=deep), :]],
                axis=1,
            ).astype(jnp.bfloat16)
            product = jnp.dot(mix[part * deep + i], inner, preferred_element_type=jnp.float32)
            outer = product[0:shards] + product[shards:2 * shards] + product[2 * shards:3 * shards]
            out_left[pl.ds(i, shards, stride=deep), :] = outer[:, :half]
            out_right[pl.ds(i, shards, stride=deep), :] = outer[:, half:]
            return carry

        lax.fori_loop(0, deep, sample_step, 0)
        both = jnp.concatenate([out_left[...], out_right[...]], axis=1)
        send2[part] = both.astype(jnp.bfloat16).reshape(shards, deep, width)

        for spot in SPOTS if line == 6 else range(line):
            send_spot(send2, recv2, send2_sem, recv2_sem, part, spot)
        recv2[part, me] = send2[part, me]

    mix_part(0)

    ordered = jnp.concatenate([ids_col[part].reshape(part_rows, 8) for part in range(PARTS)], axis=0)
    ids_row[...] = ordered.T
    loads[4].wait()
    loads[5].wait()
    state_col[...] = jnp.broadcast_to(state_ref[...], (128, rows)).T
    acc = jnp.int32(0)
    for h in range(groups):
        starts[h] = acc
        acc = acc + counts_ref[0, h]
    lane = lax.broadcasted_iota(jnp.int32, (rows, 128), 1)
    first, second, third = (piece.astype(jnp.float32) for piece in split_three(state_col[...]))
    state_parts[...] = jnp.where(
        lane == 0, first, jnp.where(lane == 1, second, jnp.where(lane == 2, third, 0.0))
    ).astype(jnp.bfloat16)

    band = 4 if groups % 4 == 0 else groups
    tall = band * CAP

    def goals(block):
        place = lax.broadcasted_iota(jnp.int32, (CAP, 128), 0)
        pieces = []
        for turn in range(band):
            other = dest(block * band + turn)
            pieces.append(jnp.where(place < counts_ref[0, other], place + starts[other], -2))
        return jnp.concatenate(pieces, axis=0)[:, 0:1]

    def count_hits(goal, size):
        total = jnp.zeros((size, samples), jnp.float32)
        for j in range(slots):
            total = total + jnp.where(ids_row[j:j + 1, :] == goal, 1.0, 0.0)
        return total.astype(jnp.bfloat16)

    def pick_step(block, carry):
        here = pl.ds(pl.multiple_of(block * tall, tall), tall)
        goal = goals(block)
        for piece in range(2):
            span = slice(piece * tall // 2, (piece + 1) * tall // 2)
            at = pl.ds(pl.multiple_of(block * tall + piece * tall // 2, tall // 2), tall // 2)
            picked_hit[at, :] = count_hits(goal[span], tall // 2)
        pick = jnp.where(
            goal == lax.broadcasted_iota(jnp.int32, (tall, rows), 1), 1.0, 0.0
        ).astype(jnp.bfloat16)
        product = jnp.dot(pick, parts[...], preferred_element_type=jnp.float32)
        both = product[:, 0:width] + product[:, width:2 * width]
        picked_table[here, :] = both + product[:, 2 * width:3 * width]
        product = jnp.dot(pick, state_parts[...], preferred_element_type=jnp.float32)
        total = (product[:, 0:1] + product[:, 1:2]) + product[:, 2:3]
        picked_state[here, :] = jnp.broadcast_to(total, (tall, 128))
        return carry

    lax.fori_loop(0, groups // band, pick_step, 0)

    mix_part(1)

    row_block = 128 if rows % 128 == 0 else rows

    def hit_step(block, carry):
        base = pl.multiple_of(block * row_block, row_block)
        row = lax.broadcasted_iota(jnp.int32, (row_block, samples), 0) + base
        hit[pl.ds(base, row_block), :] = count_hits(row, row_block)
        return carry

    lax.fori_loop(0, rows // row_block, hit_step, 0)
    side_send[...] = jnp.zeros(side_send.shape, jnp.float32)

    all_blocks(send2, recv2, send2_sem, recv2_sem, 0).wait_recv()
    returned = recv2[0].reshape(part_rows, width)
    picked_grads[...] = jnp.dot(
        picked_hit[:, 0:part_rows], returned, preferred_element_type=jnp.float32
    )
    grads[...] = jnp.dot(hit[:, 0:part_rows], returned, preferred_element_type=jnp.float32)

    def adagrad(old_rows, old_state, row_grads):
        square = jnp.sum(row_grads * row_grads, axis=-1, keepdims=True) * (1.0 / width)
        new_state = old_state + square
        step = learn_rate / (jnp.sqrt(new_state) + epsilon)
        return old_rows - row_grads * step[:, 0:1], new_state

    def code_copy(other):
        return pltpu.make_async_remote_copy(
            src_ref=code_send.at[other],
            dst_ref=code_recv.at[group],
            send_sem=code_sem.at[0],
            recv_sem=code_sem.at[1],
            device_id=(other, me),
            device_id_type=MESH,
        )

    def side_copy(other):
        return pltpu.make_async_remote_copy(
            src_ref=side_send.at[other],
            dst_ref=side_recv.at[group],
            send_sem=side_sem.at[0],
            recv_sem=side_sem.at[1],
            device_id=(other, me),
            device_id_type=MESH,
        )

    all_blocks(send2, recv2, send2_sem, recv2_sem, 1).wait_recv()

    def pack_step(block, carry):
        here = pl.ds(pl.multiple_of(block * tall, tall), tall)
        row_grads = picked_grads[here, :] + jnp.dot(
            picked_hit[here, part_rows:2 * part_rows],
            recv2[1].reshape(part_rows, width),
            preferred_element_type=jnp.float32,
        )
        new_rows, new_state = adagrad(picked_table[here, :], picked_state[here, :], row_grads)
        scale = jnp.maximum(jnp.max(jnp.abs(new_rows), axis=-1, keepdims=True), 1e-30)
        values = jnp.round(new_rows * (TOP / scale))
        values = values.astype(jnp.int32).astype(jnp.int16).reshape(band, CAP, width)
        at = lax.broadcasted_iota(jnp.int32, (tall, 128), 1)
        aside = jnp.where(at == 0, new_state, scale * (1.0 / TOP)).T
        for turn in range(band):
            k = block * band + turn
            other = dest(k)
            code_send[other] = values[turn]
            side_send[other, :, 0:CAP] = aside[0:2, turn * CAP:(turn + 1) * CAP]

            @pl.when(other != group)
            def _():
                code_copy(other).start()
                side_copy(other).start()

        return carry

    lax.fori_loop(0, groups // band, pack_step, 0)
    stores = [
        pltpu.make_async_copy(source, target, store_sem.at[i])
        for i, (source, target) in enumerate((
            (code_send.at[group], code_recv.at[group]),
            (side_send.at[group], side_recv.at[group]),
            (new_table_ref, new_table_hbm),
            (new_state_ref, new_state_hbm),
        ))
    ]
    stores[0].start()
    stores[1].start()

    def update_step(block, carry):
        base = pl.multiple_of(block * row_block, row_block)
        here = pl.ds(base, row_block)
        row_grads = grads[here, :] + jnp.dot(
            hit[here, part_rows:2 * part_rows],
            recv2[1].reshape(part_rows, width),
            preferred_element_type=jnp.float32,
        )
        new_rows, new_state = adagrad(table_ref[here, :], state_col[here, :], row_grads)
        new_table_ref[here, :] = new_rows
        new_col[here, :] = new_state
        return carry

    lax.fori_loop(0, rows // row_block, update_step, 0)
    stores[2].start()
    new_state_ref[...] = new_col[...].T[0:1]
    stores[3].start()

    others = pl.ds(0, groups - 1)
    next_group = (group + 1) % groups
    all_codes = pltpu.make_async_remote_copy(
        src_ref=code_send.at[others],
        dst_ref=code_recv.at[others],
        send_sem=code_sem.at[0],
        recv_sem=code_sem.at[1],
        device_id=(next_group, me),
        device_id_type=MESH,
    )
    all_sides = pltpu.make_async_remote_copy(
        src_ref=side_send.at[others],
        dst_ref=side_recv.at[others],
        send_sem=side_sem.at[0],
        recv_sem=side_sem.at[1],
        device_id=(next_group, me),
        device_id_type=MESH,
    )
    for part in range(PARTS):
        all_blocks(send1, recv1, send1_sem, recv1_sem, part).wait_send()
        all_blocks(send2, recv2, send2_sem, recv2_sem, part).wait_send()
    for store in stores:
        store.wait()
    all_sides.wait_send()
    all_codes.wait_send()
    all_sides.wait_recv()
    all_codes.wait_recv()


def finish_kernel(
    table_hbm, state_hbm, code_hbm, side_hbm,
    new_table_ref, new_state_ref, arrived_ref, arrived_state_ref,
    table_ref, state_ref, code_ref, side_ref, decoded, states, in_sems, out_sems,
):
    groups = code_ref.shape[0]
    pieces = 4
    band = groups // pieces
    rows = table_ref.shape[2] // pieces
    loads = [
        pltpu.make_async_copy(side_hbm, side_ref, in_sems.at[0]),
        pltpu.make_async_copy(state_hbm, state_ref.at[0], in_sems.at[1]),
    ]
    for block in range(pieces):
        here = pl.ds(block * band, band)
        loads.append(
            pltpu.make_async_copy(code_hbm.at[here], code_ref.at[here], in_sems.at[2 + block])
        )
    for block in range(pieces):
        here = pl.ds(block * rows, rows)
        loads.append(
            pltpu.make_async_copy(
                table_hbm.at[here], table_ref.at[0, 0, here], in_sems.at[2 + pieces + block]
            )
        )
    for load in loads:
        load.start()
    stores = []

    def store(source, target):
        copy = pltpu.make_async_copy(source, target, out_sems.at[len(stores)])
        copy.start()
        stores.append(copy)

    loads[0].wait()
    states[0] = side_ref[:, 0:1, 0:CAP]
    store(states, arrived_state_ref)
    scales = side_ref[:, 1, :].T
    loads[1].wait()
    store(state_ref, new_state_ref)
    for block in range(pieces):
        loads[2 + block].wait()
        for turn in range(band):
            h = block * band + turn
            decoded[0, h, 0] = code_ref[h].astype(jnp.float32) * scales[0:CAP, h:h + 1]
        here = pl.ds(block * band, band)
        store(decoded.at[0, here], arrived_ref.at[0, here])
    for block in range(pieces):
        here = pl.ds(block * rows, rows)
        loads[2 + pieces + block].wait()
        store(table_ref.at[0, 0, here], new_table_ref.at[0, 0, here])
    for copy in stores:
        copy.wait()


def on_device(table, row_state, bag_ids, bag_lengths, interaction_grad, move_rows):
    groups = lax.axis_size("group")
    shards = lax.axis_size("shard")
    line = 6 if shards % 6 == 0 else 2
    rows, width = table.shape[2:]
    slots, samples = bag_ids.shape[2:]
    deep = samples // shards // PARTS
    squares = jnp.transpose(interaction_grad[0], (0, 2, 1)).reshape(samples, shards)
    in_hbm = pl.BlockSpec(memory_space=pltpu.HBM)
    blocks = (PARTS, shards, deep, width)
    bf16, f32, i32, i16 = jnp.bfloat16, jnp.float32, jnp.int32, jnp.int16
    lanes = (shards * deep, width // 2)
    moved = groups * CAP
    pair = pltpu.SemaphoreType.DMA((2,))
    new_table, new_state, code, side = pl.pallas_call(
        functools.partial(bag_kernel, groups, shards, line),
        name="bags",
        out_shape=(
            jax.ShapeDtypeStruct((rows, width), f32),
            jax.ShapeDtypeStruct((1, rows), f32),
            jax.ShapeDtypeStruct((groups, CAP, width), i16),
            jax.ShapeDtypeStruct((groups, 2, 128), f32),
        ),
        in_specs=[in_hbm] * 6,
        out_specs=(in_hbm,) * 4,
        scratch_shapes=[
            pltpu.VMEM((rows, width), f32),
            pltpu.VMEM((1, rows), f32),
            pltpu.VMEM((slots, samples), i32),
            pltpu.VMEM((1, samples), i32),
            pltpu.VMEM((samples, shards), f32),
            pltpu.SMEM((1, groups), i32),
            pltpu.VMEM((PARTS, shards // line, line, deep, 8), i32),
            pltpu.VMEM((8, samples), i32),
            pltpu.VMEM((rows, 3 * width), bf16),
            pltpu.VMEM((rows, 128), bf16),
            pltpu.VMEM((rows, samples), bf16),
            pltpu.VMEM((moved, samples), bf16),
            pltpu.VMEM((PARTS * deep, 3 * shards, shards), bf16),
            pltpu.VMEM(blocks, bf16),
            pltpu.VMEM(blocks, bf16),
            pltpu.VMEM(blocks, bf16),
            pltpu.VMEM(blocks, bf16),
            pltpu.VMEM(lanes, f32),
            pltpu.VMEM(lanes, f32),
            pltpu.VMEM(lanes, f32),
            pltpu.VMEM(lanes, f32),
            pltpu.VMEM((rows, width), f32),
            pltpu.VMEM((moved, width), f32),
            pltpu.VMEM((moved, width), f32),
            pltpu.VMEM((moved, 128), f32),
            pltpu.VMEM((rows, 128), f32),
            pltpu.VMEM((rows, 128), f32),
            pltpu.VMEM((rows, width), f32),
            pltpu.VMEM((1, rows), f32),
            pltpu.VMEM((groups, CAP, width), i16),
            pltpu.VMEM((groups, 2, 128), f32),
            pltpu.SMEM((groups,), i32),
            pltpu.SemaphoreType.DMA((6,)),
            pltpu.SemaphoreType.DMA((4,)),
            pair, pair, pair, pair, pair, pair,
        ],
        compiler_params=pltpu.CompilerParams(
            collective_id=0, has_side_effects=True, vmem_limit_bytes=VMEM_BYTES
        ),
        cost_estimate=pl.CostEstimate(
            flops=12 * samples * rows * width, bytes_accessed=6 * rows * width * 4, transcendentals=0
        ),
    )(
        table[0, 0],
        row_state[0],
        bag_ids[0, 0],
        bag_lengths[0],
        squares,
        move_rows[0],
    )
    return pl.pallas_call(
        finish_kernel,
        name="finish",
        out_shape=(
            jax.ShapeDtypeStruct((1, 1, rows, width), f32),
            jax.ShapeDtypeStruct((1, 1, rows), f32),
            jax.ShapeDtypeStruct((1, groups, 1, CAP, width), f32),
            jax.ShapeDtypeStruct((1, groups, 1, CAP), f32),
        ),
        in_specs=[in_hbm] * 4,
        out_specs=(in_hbm,) * 4,
        scratch_shapes=[
            pltpu.VMEM((1, 1, rows, width), f32),
            pltpu.VMEM((1, 1, rows), f32),
            pltpu.VMEM((groups, CAP, width), i16),
            pltpu.VMEM((groups, 2, 128), f32),
            pltpu.VMEM((1, groups, 1, CAP, width), f32),
            pltpu.VMEM((1, groups, 1, CAP), f32),
            pltpu.SemaphoreType.DMA((10,)),
            pltpu.SemaphoreType.DMA((10,)),
        ],
        compiler_params=pltpu.CompilerParams(vmem_limit_bytes=VMEM_BYTES),
        cost_estimate=pl.CostEstimate(
            flops=rows * width, bytes_accessed=10 * rows * width, transcendentals=0
        ),
    )(new_table, new_state, code, side)


def solution(mesh):
    in_specs = (
        P("group", "shard", None, None),
        P("group", "shard", None),
        P("group", "shard", None, None),
        P("group", "shard", None),
        P("group", None, None, "shard"),
        P("group", "shard", None),
    )
    out_specs = (
        P("group", "shard", None, None),
        P("group", "shard", None),
        P("group", None, "shard", None, None),
        P("group", None, "shard", None),
    )
    return jax.shard_map(
        on_device, mesh=mesh, in_specs=in_specs, out_specs=out_specs, check_vma=False
    )
```
